32 devices in a mesh: users: 8 (over z, x), items: 4 (over y, core).
Axes of the slice: x: 2, y: 2, z: 4, core: 2. Of those that a mesh axis runs over, the one named last changes fastest.
Arguments:
- user_factors: bfloat16 [65536, 256], P(('users', 'items')), may hold values from -1.5 to 1.5
- item_factors: bfloat16 [1024, 256], P('items'), may hold values from -1.5 to 1.5
- block_user: int32 [32, 128], P(('users', 'items')), may hold values from 0 to 15
- block_item: int32 [32, 128], P(('users', 'items')), may hold values from 0 to 7
- counts: int32 [32], P(('users', 'items')), may hold values from 1 to 128, as said below
- ratings: bfloat16 [32, 128, 128, 128], P(('users', 'items')), may hold values from -6 to 6
- weights: bfloat16 [32, 128, 128, 128], P(('users', 'items')), may hold values from 0 to 4
Outputs:
- user_grad: float32 [65536, 256], P(('users', 'items'))
- item_grad: float32 [1024, 256], P(('users', 'items'))
The draws below stay inside these ranges and needn't reach their ends.
Inputs may be any that keep to these rules, and one draw needn't show every extreme that they name: counts[g] live slots come first on device g; later slots are ignored; some device has exactly 128 and some device exactly 1.
All inputs are finite; a program needn't handle non-finite values.
Results may differ from the reference program's by a relative error of at most 0.0022.
Values may be sent and summed in bfloat16 or wider, within the bound.
No kernel may reach another device: no remote copies, remote signals or barrier semaphores. Data moves between devices by JAX's collectives and lax.ppermute only.
A program may use at most 64 MiB of HBM per device.

```python
import jax
import jax.numpy as jnp
from jax import lax

RANK = 256
BLK = 128
UBLK_DEV = 16
NB = 128
GROUPS = 32
USERS = 65536
IBLK = 8
ITEMS = 1024


def draw_counts(key, part):
    first_key, second_key, third_key = jax.random.split(key, 3)
    values = jax.random.randint(first_key, (GROUPS,), 1, NB + 1)
    position = jax.random.randint(second_key, (), 0, GROUPS)
    offset = jax.random.randint(third_key, (), 1, GROUPS)
    other = (position + offset) % GROUPS
    values = values.at[position].set(NB)
    values = values.at[other].set(1)
    return values.astype(jnp.int32)


def draw_weights(key, part):
    first_key, second_key = jax.random.split(key)
    shape = (GROUPS, NB, BLK, BLK)
    observed = jax.random.bernoulli(first_key, 0.5, shape)
    magnitude = jnp.exp(jax.random.uniform(second_key, shape, jnp.float32, jnp.log(0.25), jnp.log(4.0)))
    return jnp.where(observed, magnitude, 0.0).astype(jnp.float32).astype(jnp.bfloat16)


def place_ends(result, key, low, top_value):
    longest = result.shape.index(max(result.shape))
    spots = []
    for shift in (0, 1):
        where = [jax.random.randint(jax.random.fold_in(key, axis), (), 0, length) for axis, length in enumerate(result.shape)]
        where[longest] = (where[longest] + shift) % result.shape[longest]
        spots.append(tuple(where))
    return result.at[spots[0]].set(low).at[spots[1]].set(top_value)


def steps_of(key, extent, shards, low, top_value):
    def one(dim, parts):
        draws = jax.random.uniform(jax.random.fold_in(jax.random.fold_in(key, 6), dim), (parts,), jnp.float32, low / len(shards), top_value / len(shards))
        return jnp.repeat(jnp.exp(draws), extent[dim] // parts).reshape((-1,) + (1,) * (len(extent) - dim - 1))

    factor_of = one(*shards[0])
    for cut in shards[1:]:
        factor_of = factor_of * one(*cut)
    return factor_of


def centred(rng, dims, width, limit, shards=(), kind=jnp.bfloat16):
    factor_of = steps_of(rng, dims, shards, -0.22, 0.18) if shards else 1.0
    drawn = jax.random.normal(rng, dims, jnp.float32) * width * factor_of
    return jnp.minimum(jnp.maximum(drawn, -limit), limit).astype(kind)


def setup_inputs(seed: int = 0) -> dict:
    arg_keys = jax.random.split(jax.random.key(seed), 8)
    user_factors = centred(arg_keys[0], (USERS, RANK), 0.25, 1.5, ((0, 32),))
    item_factors = centred(arg_keys[1], (ITEMS, RANK), 0.25, 1.5, ((0, 4),))
    block_user = place_ends(jax.random.randint(arg_keys[2], (GROUPS, NB), 0, UBLK_DEV), jax.random.fold_in(arg_keys[2], 1), 0, UBLK_DEV - 1).astype(jnp.int32)
    block_item = place_ends(jax.random.randint(arg_keys[3], (GROUPS, NB), 0, IBLK), jax.random.fold_in(arg_keys[3], 1), 0, IBLK - 1).astype(jnp.int32)
    counts = draw_counts(jax.random.fold_in(arg_keys[7], 71), 0)
    ratings = centred(arg_keys[5], (GROUPS, NB, BLK, BLK), 1.0, 6.0, ((0, 32),))
    weights = draw_weights(jax.random.fold_in(arg_keys[7], 71), 0)
    return {"user_factors": user_factors, "item_factors": item_factors, "block_user": block_user, "block_item": block_item, "counts": counts, "ratings": ratings, "weights": weights}


grad_scale = 0.015625
decay_rate = 0.05


def reference(user_factors, item_factors, block_user, block_item, counts, ratings, weights):
    slab_rows = UBLK_DEV * BLK

    def device_step(item_acc, device):
        user_slab = lax.dynamic_slice_in_dim(user_factors, device * slab_rows, slab_rows, 0).reshape(UBLK_DEV, BLK, RANK)

        def one_block(slot, carry):
            user_acc, item_sum = carry
            user_id = block_user[device, slot]
            item_id = block_item[device, slot]
            user_tile = user_slab[user_id]
            item_tile = lax.dynamic_slice_in_dim(item_factors, item_id * BLK, BLK, 0)
            predicted = jnp.dot(user_tile, item_tile.T, preferred_element_type=jnp.float32)
            weighted = (weights[device, slot].astype(jnp.float32) * (predicted - ratings[device, slot].astype(jnp.float32))).astype(jnp.bfloat16)
            user_acc = user_acc.at[user_id].add(jnp.dot(weighted, item_tile, preferred_element_type=jnp.float32))
            previous = lax.dynamic_slice_in_dim(item_sum, item_id * BLK, BLK, 0)
            updated = previous + jnp.dot(weighted.T, user_tile, preferred_element_type=jnp.float32)
            item_sum = lax.dynamic_update_slice_in_dim(item_sum, updated, item_id * BLK, 0)
            return user_acc, item_sum

        user_zero = jnp.zeros((UBLK_DEV, BLK, RANK), jnp.float32)
        user_acc, item_acc = lax.fori_loop(0, counts[device], one_block, (user_zero, item_acc))
        return item_acc, user_acc

    item_zero = jnp.zeros((ITEMS, RANK), jnp.float32)
    item_sums, user_sums = lax.scan(device_step, item_zero, jnp.arange(GROUPS, dtype=jnp.int32))
    user_grad = user_sums.reshape(USERS, RANK) * grad_scale + decay_rate * user_factors.astype(jnp.float32)
    item_grad = item_sums * grad_scale + decay_rate * item_factors.astype(jnp.float32)
    return user_grad, item_grad
```

```python
import functools

import jax
import jax.numpy as jnp
from jax import lax
from jax.experimental import pallas as pl
from jax.experimental.pallas import tpu as pltpu
from jax.sharding import PartitionSpec as P

grad_scale = 0.015625
decay_rate = 0.05
AXES = ("users", "items")
VMEM = pl.BlockSpec(memory_space=pltpu.VMEM)
SMEM = pl.BlockSpec(memory_space=pltpu.SMEM)
ANY = pl.BlockSpec(memory_space=pl.ANY)


def phases_of(device_total):
    bit_total = device_total.bit_length() - 1
    groups = [[0]]
    for bit in range(1, bit_total, 2):
        groups.append(list(range(bit, min(bit + 2, bit_total))))
    return groups


def place_of(index, groups):
    place = 0
    for group in groups:
        for bit in reversed(group):
            place = place * 2 + ((index >> bit) & 1)
    return place


def item_kernel(unroll, owner_total, groups, count_ref, place_ref, user_id_ref, item_id_ref, user_ref, turned_ref,
                item_ref, rating_ref, weight_ref, keep_ref, send_ref, weighted_ref, total):
    live = count_ref[0]
    block = rating_ref.shape[2]
    total[...] = jnp.zeros_like(total)

    def turn(index, carry):
        base = index * unroll
        predicted = []
        for step in range(unroll):
            user_row = pl.multiple_of(user_id_ref[0, base + step] * block, block)
            item_row = pl.multiple_of(item_id_ref[0, base + step] * block, block)
            predicted.append(lax.dot_general(
                user_ref[pl.ds(user_row, block), :], item_ref[pl.ds(item_row, block), :],
                (((1,), (1,)), ((), ())), preferred_element_type=jnp.float32))
        terms = []
        for step in range(unroll):
            slot = base + step
            weighted = weight_ref[0, slot].astype(jnp.float32) * (
                predicted[step] - rating_ref[0, slot].astype(jnp.float32))
            weighted = jnp.where(slot < live, weighted, 0.0).astype(jnp.bfloat16)
            weighted_ref[slot] = weighted
            terms.append(jnp.dot(turned_ref[user_id_ref[0, slot]], weighted, preferred_element_type=jnp.float32))
        for step in range(unroll):
            total[item_id_ref[0, base + step]] += terms[step]
        return carry

    lax.fori_loop(0, (live + unroll - 1) // unroll, turn, 0)
    own_place = place_ref[0]
    owned = keep_ref.shape[0] * 2 // owner_total
    half = owner_total // 2
    per_block = block // owned
    for item in range(total.shape[0]):
        rows = total[item].T
        for part in range(per_block):
            place = own_place ^ place_of(item * per_block + part, groups)
            piece = rows[part * owned:(part + 1) * owned]
            row = pl.multiple_of((place % half) * owned, owned)

            @pl.when(place < half)
            def _():
                keep_ref[pl.ds(row, owned), :] = piece

            @pl.when(place >= half)
            def _():
                send_ref[pl.ds(row, owned), :] = piece


def user_kernel(unroll, count_ref, user_id_ref, item_id_ref, user_ref, item_ref, weighted_ref, grad_ref, total, sems):
    live = count_ref[0]
    block = weighted_ref.shape[1]
    total[...] = jnp.zeros_like(total)

    def turn(index, carry):
        base = index * unroll
        terms = []
        for step in range(unroll):
            item_row = pl.multiple_of(item_id_ref[0, base + step] * block, block)
            terms.append(jnp.dot(weighted_ref[base + step], item_ref[pl.ds(item_row, block), :],
                                 preferred_element_type=jnp.float32))
        for step in range(unroll):
            user_row = pl.multiple_of(user_id_ref[0, base + step] * block, block)
            total[pl.ds(user_row, block), :] += terms[step]
        return carry

    lax.fori_loop(0, (live + unroll - 1) // unroll, turn, 0)

    def writeback(index):
        rows = pl.ds(index * block, block)
        return pltpu.make_async_copy(total.at[rows], grad_ref.at[rows], sems.at[index])

    blocks = total.shape[0] // block
    for index in range(blocks):
        rows = pl.ds(index * block, block)
        total[rows, :] = total[rows, :] * grad_scale + decay_rate * user_ref[rows, :].astype(jnp.float32)
        writeback(index).start()
    for index in range(blocks):
        writeback(index).wait()


def body(user_factors, item_factors, block_user, block_item, counts, ratings, weights):
    rank = user_factors.shape[1]
    slots, block = ratings.shape[1], ratings.shape[2]
    user_rows = user_factors.shape[0]
    device_total = lax.axis_size(AXES[0]) * lax.axis_size(AXES[1])
    me = lax.axis_index(AXES[0]) * lax.axis_size(AXES[1]) + lax.axis_index(AXES[1])
    groups = phases_of(device_total)
    unroll = 16
    item_whole = lax.all_gather(item_factors, "items", axis=0, tiled=True)
    item_rows = item_whole.shape[0]
    turned = user_factors.reshape(-1, block, rank).swapaxes(1, 2)
    own_place = place_of(me, groups).astype(jnp.int32).reshape(1)
    half_shape = jax.ShapeDtypeStruct((item_rows // 2, rank), jnp.float32)
    keep, send, weighted = pl.pallas_call(
        functools.partial(item_kernel, unroll, device_total, groups),
        out_shape=(half_shape, half_shape, jax.ShapeDtypeStruct((slots, block, block), jnp.bfloat16)),
        in_specs=[SMEM] * 4 + [VMEM] * 5,
        out_specs=(VMEM,) * 3,
        scratch_shapes=[pltpu.VMEM((item_rows // block, rank, block), jnp.float32)],
        compiler_params=pltpu.CompilerParams(vmem_limit_bytes=20 << 20),
        name="item_sums",
    )(counts, own_place, block_user, block_item, user_factors, turned, item_whole, ratings, weights)
    user_grad = pl.pallas_call(
        functools.partial(user_kernel, unroll),
        out_shape=jax.ShapeDtypeStruct((user_rows, rank), jnp.float32),
        in_specs=[SMEM] * 3 + [VMEM] * 3,
        out_specs=ANY,
        scratch_shapes=[pltpu.VMEM((user_rows, rank), jnp.float32), pltpu.SemaphoreType.DMA((user_rows // block,))],
        compiler_params=pltpu.CompilerParams(vmem_limit_bytes=20 << 20),
        cost_estimate=pl.CostEstimate(flops=2 * slots * block * block * rank, bytes_accessed=8 << 20, transcendentals=0),
        name="user_sums",
    )(counts, block_user, block_item, user_factors, item_whole, weighted)

    def permute(array, mask):
        return lax.ppermute(array, AXES, [(index, index ^ mask) for index in range(device_total)])

    partial = keep + permute(send, 1)
    for group in groups[1:]:
        ways = 1 << len(group)
        parts = partial.reshape(ways, -1, rank)
        received = []
        for way in range(1, ways):
            mask = sum(((way >> index) & 1) << bit for index, bit in enumerate(group))
            received.append(permute(parts[way], mask))
        partial = parts[0]
        for array in received:
            partial = partial + array
    owned_rows = partial.shape[0]
    own_factors = lax.dynamic_slice_in_dim(item_whole, me * owned_rows, owned_rows, 0)
    item_grad = partial * grad_scale + decay_rate * own_factors.astype(jnp.float32)
    return (user_grad, item_grad)


def solution(mesh):
    in_specs = (
        P(AXES, None),
        P("items", None),
        P(AXES, None),
        P(AXES, None),
        P(AXES),
        P(AXES, None, None, None),
        P(AXES, None, None, None),
    )
    out_specs = (P(AXES, None), P(AXES, None))
    return jax.shard_map(body, mesh=mesh, in_specs=in_specs, out_specs=out_specs, check_vma=False)
```

```python
import functools

import jax
import jax.numpy as jnp
from jax import lax
from jax.experimental import pallas as pl
from jax.experimental.pallas import tpu as pltpu
from jax.sharding import PartitionSpec as P

grad_scale = 0.015625
decay_rate = 0.05
AXES = ("users", "items")
VMEM = pl.BlockSpec(memory_space=pltpu.VMEM)
SMEM = pl.BlockSpec(memory_space=pltpu.SMEM)
HBM = pl.BlockSpec(memory_space=pltpu.HBM)


def phases_of(device_total):
    bit_total = device_total.bit_length() - 1
    groups = [[0]]
    for bit in range(1, bit_total, 2):
        groups.append(list(range(bit, min(bit + 2, bit_total))))
    return groups


def place_of(index, groups):
    place = 0
    for group in groups:
        for bit in reversed(group):
            place = place * 2 + ((index >> bit) & 1)
    return place


def add_slots(unroll, first_turn, turn_total, slot_of, valid_total, user_id_ref, item_id_ref, item_row_of, user_ref,
              turned_ref, item_ref, rating_ref, weight_ref, total, before, after):
    block = rating_ref.shape[1]

    def turn(index, carry):
        base = index * unroll
        carry = before(base, carry)
        slots = [slot_of(base + step) for step in range(unroll)]
        predicted = []
        for slot in slots:
            user_row = pl.multiple_of(user_id_ref[0, slot] * block, block)
            item_row = pl.multiple_of(item_row_of(item_id_ref[0, slot]), block)
            predicted.append(lax.dot_general(
                user_ref[pl.ds(user_row, block), :], item_ref[pl.ds(item_row, block), :],
                (((1,), (1,)), ((), ())), preferred_element_type=jnp.float32))
        tiles = []
        for step, slot in enumerate(slots):
            weighted = weight_ref[slot].astype(jnp.float32) * (
                predicted[step] - rating_ref[slot].astype(jnp.float32))
            tiles.append(jnp.where(base + step < valid_total, weighted, 0.0).astype(jnp.bfloat16))
        terms = [jnp.dot(turned_ref[user_id_ref[0, slot]], tile, preferred_element_type=jnp.float32)
                 for slot, tile in zip(slots, tiles)]
        after(base, slots, tiles)
        for slot, term in zip(slots, terms):
            total[item_id_ref[0, slot]] += term
        return carry

    return lax.fori_loop(first_turn, turn_total, turn, 0)


def near_kernel(unroll, count_ref, place_ref, user_id_ref, item_id_ref, user_ref, own_ref, pair_ref, rating_ref,
                weight_ref, total, user_total, turned_ref, factor_ref, held_rating_ref, held_weight_ref, order_ref,
                item_ref, factor_sem, rating_sems, weight_sems):
    live = count_ref[0]
    item_mask = place_ref[1]
    slots = held_rating_ref.shape[0]
    block = held_rating_ref.shape[1]
    chunks = (live + unroll - 1) // unroll
    panel_rows = own_ref.shape[0]
    near_blocks = 2 * panel_rows // block

    def copies(index):
        part = pl.ds(index * unroll, unroll)
        return (
            pltpu.make_async_copy(rating_ref.at[0, part], held_rating_ref.at[part], rating_sems.at[index]),
            pltpu.make_async_copy(weight_ref.at[0, part], held_weight_ref.at[part], weight_sems.at[index]),
        )

    factor_copy = pltpu.make_async_copy(user_ref, factor_ref, factor_sem)
    factor_copy.start()
    for index in range(slots // unroll):
        @pl.when(index < chunks)
        def _():
            for copy in copies(index):
                copy.start()

    def sort(slot, near_total):
        near = (item_id_ref[0, slot] ^ item_mask) < near_blocks
        order_ref[jnp.where(near, near_total, slots - 1 - slot + near_total)] = slot
        return near_total + near.astype(jnp.int32)

    near_total = lax.fori_loop(0, live, sort, 0)
    order_ref[slots] = near_total
    item_ref[:panel_rows, :] = own_ref[...]
    item_ref[panel_rows:, :] = pair_ref[...]
    total[...] = jnp.zeros_like(total)
    user_total[...] = jnp.zeros_like(user_total)
    factor_copy.wait()
    for index in range(turned_ref.shape[0]):
        turned_ref[index] = factor_ref[index * block:(index + 1) * block, :].T

    def wait(index, carry):
        for copy in copies(index):
            copy.wait()
        return carry

    def item_row_of(item):
        return (item ^ item_mask) % near_blocks * block

    def slot_of(position):
        return jnp.where(position < near_total, order_ref[position], 0)

    def before(base, waited):
        needed = order_ref[jnp.minimum(base + unroll, near_total) - 1] // unroll + 1
        lax.fori_loop(waited, needed, wait, 0)
        return needed

    def after(base, slot_list, tiles):
        terms = []
        for slot, tile in zip(slot_list, tiles):
            item_row = pl.multiple_of(item_row_of(item_id_ref[0, slot]), block)
            terms.append(jnp.dot(tile, item_ref[pl.ds(item_row, block), :], preferred_element_type=jnp.float32))
        for slot, term in zip(slot_list, terms):
            user_row = pl.multiple_of(user_id_ref[0, slot] * block, block)
            user_total[pl.ds(user_row, block), :] += term

    waited = add_slots(unroll, 0, (near_total + unroll - 1) // unroll, slot_of, near_total, user_id_ref, item_id_ref,
                       item_row_of, factor_ref, turned_ref, item_ref, held_rating_ref, held_weight_ref, total, before,
                       after)
    lax.fori_loop(waited, chunks, wait, 0)


def far_kernel(unroll, owner_total, groups, count_ref, place_ref, user_id_ref, item_id_ref, order_ref, user_ref,
               turned_ref, near_ref, rating_ref, weight_ref, *refs):
    panel_refs, (keep_ref, send_ref, weighted_ref, item_ref, total) = refs[:-5], refs[-5:]
    slots = rating_ref.shape[0]
    block = rating_ref.shape[1]
    item_mask = place_ref[1]
    far_total = count_ref[0] - order_ref[slots]
    row = 0
    for panel_ref in panel_refs:
        item_ref[row:row + panel_ref.shape[0], :] = panel_ref[...]
        row += panel_ref.shape[0]
    total[...] = near_ref[...]

    def slot_of(position):
        return jnp.where(position < far_total, order_ref[slots - 1 - position], 0)

    def after(base, slot_list, tiles):
        for step, tile in enumerate(tiles):
            weighted_ref[base + step] = tile

    add_slots(unroll, 0, (far_total + unroll - 1) // unroll, slot_of, far_total, user_id_ref, item_id_ref,
              lambda item: (item ^ item_mask) * block, user_ref, turned_ref, item_ref, rating_ref, weight_ref, total,
              lambda base, carry: carry, after)
    own_place = place_ref[0]
    owned = keep_ref.shape[0] * 2 // owner_total
    half = owner_total // 2
    per_block = block // owned
    for item in range(total.shape[0]):
        rows = total[item].T
        for part in range(per_block):
            place = own_place ^ place_of(item * per_block + part, groups)
            piece = rows[part * owned:(part + 1) * owned]
            row = pl.multiple_of((place % half) * owned, owned)

            @pl.when(place < half)
            def _():
                keep_ref[pl.ds(row, owned), :] = piece

            @pl.when(place >= half)
            def _():
                send_ref[pl.ds(row, owned), :] = piece


def user_kernel(unroll, count_ref, place_ref, user_id_ref, item_id_ref, order_ref, near_ref, item_ref, user_ref,
                weighted_ref, grad_ref, total_ref, sems):
    slots = weighted_ref.shape[0]
    block = weighted_ref.shape[1]
    item_mask = place_ref[1]
    far_total = count_ref[0] - order_ref[slots]
    total_ref[...] = near_ref[...]

    def turn(index, carry):
        base = index * unroll
        chosen = [jnp.where(base + step < far_total, order_ref[slots - 1 - base - step], 0) for step in range(unroll)]
        terms = []
        for step, slot in enumerate(chosen):
            item_row = pl.multiple_of((item_id_ref[0, slot] ^ item_mask) * block, block)
            terms.append(jnp.dot(weighted_ref[base + step], item_ref[pl.ds(item_row, block), :],
                                 preferred_element_type=jnp.float32))
        for slot, term in zip(chosen, terms):
            user_row = pl.multiple_of(user_id_ref[0, slot] * block, block)
            total_ref[pl.ds(user_row, block), :] += term
        return carry

    lax.fori_loop(0, (far_total + unroll - 1) // unroll, turn, 0)

    def writeback(index):
        rows = pl.ds(index * block, block)
        return pltpu.make_async_copy(total_ref.at[rows], grad_ref.at[rows], sems.at[index])

    blocks = total_ref.shape[0] // block
    for index in range(blocks):
        rows = pl.ds(index * block, block)
        total_ref[rows, :] = total_ref[rows, :] * grad_scale + decay_rate * user_ref[rows, :].astype(jnp.float32)
        writeback(index).start()
    for index in range(blocks):
        writeback(index).wait()


def body(user_factors, item_factors, block_user, block_item, counts, ratings, weights):
    rank = user_factors.shape[1]
    slots, block = ratings.shape[1], ratings.shape[2]
    user_rows = user_factors.shape[0]
    panel_rows = item_factors.shape[0]
    panel_total = lax.axis_size("items")
    device_total = lax.axis_size("users") * panel_total
    panel_index = lax.axis_index("items")
    me = lax.axis_index("users") * panel_total + panel_index
    groups = phases_of(device_total)
    unroll = 16
    item_rows = panel_rows * panel_total

    def permute(array, mask):
        return lax.ppermute(array, AXES, [(index, index ^ mask) for index in range(device_total)])

    def estimate(micros):
        return pl.CostEstimate(flops=0, bytes_accessed=int(3e6 * micros), transcendentals=0)

    panels = [item_factors] + [permute(item_factors, mask) for mask in range(1, panel_total)]
    places = jnp.stack([place_of(me, groups), panel_index * (panel_rows // block)]).astype(jnp.int32)
    held = jax.ShapeDtypeStruct((slots, block, block), jnp.bfloat16)
    sums_shape = jax.ShapeDtypeStruct((item_rows // block, rank, block), jnp.float32)
    user_shape = jax.ShapeDtypeStruct((user_rows, rank), jnp.float32)
    near_sums, near_users, turned, factors, held_ratings, held_weights, order = pl.pallas_call(
        functools.partial(near_kernel, unroll),
        out_shape=(
            sums_shape,
            user_shape,
            jax.ShapeDtypeStruct((user_rows // block, rank, block), jnp.bfloat16),
            jax.ShapeDtypeStruct((user_rows, rank), jnp.bfloat16),
            held,
            held,
            jax.ShapeDtypeStruct((slots + 8,), jnp.int32),
        ),
        in_specs=[SMEM] * 4 + [HBM] + [VMEM] * 2 + [HBM] * 2,
        out_specs=(VMEM,) * 6 + (SMEM,),
        scratch_shapes=[pltpu.VMEM((2 * panel_rows, rank), jnp.bfloat16), pltpu.SemaphoreType.DMA]
        + [pltpu.SemaphoreType.DMA((slots // unroll,))] * 2,
        compiler_params=pltpu.CompilerParams(vmem_limit_bytes=37 << 20),
        cost_estimate=estimate(8),
        name="near_sums",
    )(counts, places, block_user, block_item, user_factors, panels[0], panels[1], ratings, weights)

    half_shape = jax.ShapeDtypeStruct((item_rows // 2, rank), jnp.float32)
    keep, send, weighted, item_whole = pl.pallas_call(
        functools.partial(far_kernel, unroll, device_total, groups),
        out_shape=(half_shape, half_shape, held, jax.ShapeDtypeStruct((item_rows, rank), jnp.bfloat16)),
        in_specs=[SMEM] * 5 + [VMEM] * (5 + panel_total),
        out_specs=(VMEM,) * 4,
        scratch_shapes=[pltpu.VMEM(sums_shape.shape, jnp.float32)],
        compiler_params=pltpu.CompilerParams(vmem_limit_bytes=12 << 20),
        cost_estimate=estimate(5),

        name="far_sums",
    )(counts, places, block_user, block_item, order, factors, turned, near_sums, held_ratings, held_weights, *panels)

    partial = keep + permute(send, 1)
    user_grad = pl.pallas_call(
        functools.partial(user_kernel, unroll),
        out_shape=user_shape,
        in_specs=[SMEM] * 5 + [VMEM] * 4,
        out_specs=HBM,
        scratch_shapes=[pltpu.VMEM(user_shape.shape, user_shape.dtype),
                        pltpu.SemaphoreType.DMA((user_rows // block,))],
        compiler_params=pltpu.CompilerParams(vmem_limit_bytes=12 << 20),
        cost_estimate=estimate(3),
        name="user_sums",
    )(counts, places, block_user, block_item, order, near_users, item_whole, factors, weighted)
    for group in groups[1:]:
        ways = 1 << len(group)
        parts = partial.reshape(ways, -1, rank)
        partial = parts[0]
        for way in reversed(range(1, ways)):
            mask = sum(((way >> index) & 1) << bit for index, bit in enumerate(group))
            partial = partial + permute(parts[way], mask)
    owned_rows = partial.shape[0]
    own_row = (me * owned_rows) ^ (panel_index * panel_rows)
    own_factors = lax.dynamic_slice_in_dim(item_whole, own_row, owned_rows, 0)
    item_grad = partial * grad_scale + decay_rate * own_factors.astype(jnp.float32)
    return (user_grad, item_grad)


def solution(mesh):
    in_specs = (
        P(AXES, None),
        P("items", None),
        P(AXES, None),
        P(AXES, None),
        P(AXES),
        P(AXES, None, None, None),
        P(AXES, None, None, None),
    )
    out_specs = (P(AXES, None), P(AXES, None))
    return jax.shard_map(body, mesh=mesh, in_specs=in_specs, out_specs=out_specs, check_vma=False)
```

```python
import functools

import jax
import jax.numpy as jnp
from jax import lax
from jax.experimental import pallas as pl
from jax.experimental.pallas import tpu as pltpu
from jax.sharding import PartitionSpec as P

grad_scale = 0.015625
decay_rate = 0.05
AXES = ("users", "items")
UNROLL = 16
VMEM = pl.BlockSpec(memory_space=pltpu.VMEM)
SMEM = pl.BlockSpec(memory_space=pltpu.SMEM)
HBM = pl.BlockSpec(memory_space=pltpu.HBM)


def phases_of(device_total):
    bit_total = device_total.bit_length() - 1
    groups = [[0]]
    for bit in range(1, bit_total, 2):
        groups.append(list(range(bit, min(bit + 2, bit_total))))
    return groups


def place_of(index, groups):
    place = 0
    for group in groups:
        for bit in reversed(group):
            place = place * 2 + ((index >> bit) & 1)
    return place


def order_kernel(entry_ref, order_ref, *, slots, near_blocks):
    stride = order_ref.shape[0] // 2
    live = entry_ref[slots]

    def sort(slot, near_total):
        entry = entry_ref[slot]
        near = (entry // 256) % 256 < near_blocks
        order_ref[jnp.where(near, near_total, stride + slot - near_total)] = entry
        return near_total + near.astype(jnp.int32)

    near_total = lax.fori_loop(0, live, sort, 0)

    def pad(index, carry):
        order_ref[near_total + index] = 0
        order_ref[stride + live - near_total + index] = 0
        return carry

    lax.fori_loop(0, UNROLL, pad, 0)
    order_ref[stride - 1] = near_total
    order_ref[2 * stride - 1] = live - near_total
    order_ref[2 * stride - 2] = entry_ref[slots + 1]


def fields(entry, block):
    return pl.multiple_of(entry // 65536 * block, block), (entry // 256) % 256, entry % 256


def add_slots(first, total_slots, order_ref, user_ref, turned_ref, item_ref, rating_ref, weight_ref, held_rating,
              held_weight, rating_sems, weight_sems, total, after):
    block = held_rating.shape[1]
    turns = (total_slots + UNROLL - 1) // UNROLL
    ahead = 3

    def start(index):
        for step in range(UNROLL):
            position = index * UNROLL + step
            slot = fields(order_ref[first + position], block)[2]
            pltpu.make_async_copy(rating_ref.at[0, slot], held_rating.at[position], rating_sems.at[index]).start()
            pltpu.make_async_copy(weight_ref.at[0, slot], held_weight.at[position], weight_sems.at[index]).start()

    def wait(index):
        part = pl.ds(index * UNROLL, UNROLL)
        pltpu.make_async_copy(rating_ref.at[0, pl.ds(0, UNROLL)], held_rating.at[part], rating_sems.at[index]).wait()
        pltpu.make_async_copy(weight_ref.at[0, pl.ds(0, UNROLL)], held_weight.at[part], weight_sems.at[index]).wait()

    def prime(index, carry):
        start(index)
        return carry

    def turn(index, carry):
        @pl.when(index + ahead < turns)
        def _():
            start(index + ahead)

        wait(index)
        base = index * UNROLL
        chosen = [fields(order_ref[first + base + step], block) for step in range(UNROLL)]
        predicted = []
        for user_row, item, _ in chosen:
            item_row = pl.multiple_of(item * block, block)
            predicted.append(lax.dot_general(
                user_ref[pl.ds(user_row, block), :], item_ref[pl.ds(item_row, block), :],
                (((1,), (1,)), ((), ())), preferred_element_type=jnp.float32))
        tiles = []
        for step in range(UNROLL):
            weighted = held_weight[base + step].astype(jnp.float32) * (
                predicted[step] - held_rating[base + step].astype(jnp.float32))
            tiles.append(jnp.where(base + step < total_slots, weighted, 0.0).astype(jnp.bfloat16))
        terms = [jnp.dot(turned_ref[entry[0] // block], tile, preferred_element_type=jnp.float32)
                 for entry, tile in zip(chosen, tiles)]
        after(index, chosen, tiles)
        for (_, item, _), term in zip(chosen, terms):
            total[item] += term
        return carry

    def prepare():
        lax.fori_loop(0, jnp.minimum(turns, ahead), prime, 0)

    def run():
        lax.fori_loop(0, turns, turn, 0)

    return prepare, run


def near_kernel(order_ref, user_ref, own_ref, pair_ref, rating_ref, weight_ref, total, user_total, turned_ref,
                held_rating, held_weight, item_ref, rating_sems, weight_sems):
    block = held_rating.shape[1]
    stride = order_ref.shape[0] // 2
    near_total = order_ref[stride - 1]

    def after(index, chosen, tiles):
        terms = []
        for (_, item, _), tile in zip(chosen, tiles):
            item_row = pl.multiple_of(item * block, block)
            terms.append(jnp.dot(tile, item_ref[pl.ds(item_row, block), :], preferred_element_type=jnp.float32))
        for (user_row, _, _), term in zip(chosen, terms):
            user_total[pl.ds(user_row, block), :] += term

    prepare, run = add_slots(0, near_total, order_ref, user_ref, turned_ref, item_ref, rating_ref, weight_ref,
                             held_rating, held_weight, rating_sems, weight_sems, total, after)
    prepare()
    item_ref[:own_ref.shape[0], :] = own_ref[...]
    item_ref[own_ref.shape[0]:, :] = pair_ref[...]
    total[...] = jnp.zeros_like(total)
    user_total[...] = jnp.zeros_like(user_total)
    for index in range(turned_ref.shape[0]):
        turned_ref[index] = user_ref[index * block:(index + 1) * block, :].T
    run()


def join(panel_refs, item_ref):
    row = 0
    for panel_ref in panel_refs:
        item_ref[row:row + panel_ref.shape[0], :] = panel_ref[...]
        row += panel_ref.shape[0]


def far_kernel(owner_total, groups, order_ref, user_ref, turned_ref, near_ref, rating_ref, weight_ref, *refs):
    panel_refs, refs = refs[:-11], refs[-11:]
    (keep_ref, send_ref, weighted_ref, held_rating, held_weight, item_ref, total, tile_ref, rating_sems,
     weight_sems, tile_sems) = refs
    block = held_rating.shape[1]
    stride = order_ref.shape[0] // 2
    far_total = order_ref[2 * stride - 1]
    turns = (far_total + UNROLL - 1) // UNROLL

    def copy_of(index):
        part = pl.ds(index * UNROLL, UNROLL)
        return pltpu.make_async_copy(tile_ref.at[part], weighted_ref.at[part], tile_sems.at[index])

    def after(index, chosen, tiles):
        for step, tile in enumerate(tiles):
            tile_ref[index * UNROLL + step] = tile
        copy_of(index).start()

    prepare, run = add_slots(stride, far_total, order_ref, user_ref, turned_ref, item_ref, rating_ref, weight_ref,
                             held_rating, held_weight, rating_sems, weight_sems, total, after)
    prepare()
    join(panel_refs, item_ref)
    total[...] = near_ref[...]
    run()
    own_place = order_ref[2 * stride - 2]
    owned = keep_ref.shape[0] * 2 // owner_total
    half = owner_total // 2
    per_block = block // owned
    for item in range(total.shape[0]):
        rows = total[item].T
        for part in range(per_block):
            place = own_place ^ place_of(item * per_block + part, groups)
            piece = rows[part * owned:(part + 1) * owned]
            row = pl.multiple_of((place % half) * owned, owned)

            @pl.when(place < half)
            def _():
                keep_ref[pl.ds(row, owned), :] = piece

            @pl.when(place >= half)
            def _():
                send_ref[pl.ds(row, owned), :] = piece

    def finish(index, carry):
        copy_of(index).wait()
        return carry

    lax.fori_loop(0, turns, finish, 0)


def user_kernel(order_ref, user_ref, near_ref, weighted_ref, *refs):
    panel_refs, (grad_ref, token_ref, tile_ref, item_ref, total_ref, tile_sems, sems) = refs[:-7], refs[-7:]
    block = tile_ref.shape[1]
    stride = order_ref.shape[0] // 2
    far_total = order_ref[2 * stride - 1]
    turns = (far_total + UNROLL - 1) // UNROLL

    def copy_of(index):
        part = pl.ds(index * UNROLL, UNROLL)
        return pltpu.make_async_copy(weighted_ref.at[part], tile_ref.at[part], tile_sems.at[index])

    def prime(index, carry):
        copy_of(index).start()
        return carry

    lax.fori_loop(0, turns, prime, 0)
    token_ref[...] = jnp.zeros_like(token_ref)
    join(panel_refs, item_ref)
    total_ref[...] = near_ref[...]

    def turn(index, carry):
        copy_of(index).wait()
        base = index * UNROLL
        chosen = [fields(order_ref[stride + base + step], block) for step in range(UNROLL)]
        terms = []
        for step, (_, item, _) in enumerate(chosen):
            item_row = pl.multiple_of(item * block, block)
            terms.append(jnp.dot(tile_ref[base + step], item_ref[pl.ds(item_row, block), :],
                                 preferred_element_type=jnp.float32))
        for (user_row, _, _), term in zip(chosen, terms):
            total_ref[pl.ds(user_row, block), :] += term
        return carry

    lax.fori_loop(0, turns, turn, 0)

    def writeback(index):
        rows = pl.ds(index * block, block)
        return pltpu.make_async_copy(total_ref.at[rows], grad_ref.at[rows], sems.at[index])

    blocks = total_ref.shape[0] // block
    for index in range(blocks):
        rows = pl.ds(index * block, block)
        total_ref[rows, :] = total_ref[rows, :] * grad_scale + decay_rate * user_ref[rows, :].astype(jnp.float32)
        writeback(index).start()
    for index in range(blocks):
        writeback(index).wait()


def body(user_factors, item_factors, block_user, block_item, counts, ratings, weights):
    rank = user_factors.shape[1]
    slots, block = ratings.shape[1], ratings.shape[2]
    user_rows = user_factors.shape[0]
    panel_rows = item_factors.shape[0]
    panel_total = lax.axis_size("items")
    device_total = lax.axis_size("users") * panel_total
    panel_index = lax.axis_index("items")
    me = lax.axis_index("users") * panel_total + panel_index
    groups = phases_of(device_total)
    item_rows = panel_rows * panel_total
    turns = slots // UNROLL

    def permute(array, mask):
        return lax.ppermute(array, AXES, [(index, index ^ mask) for index in range(device_total)])

    def options(micros):
        return dict(
            compiler_params=pltpu.CompilerParams(vmem_limit_bytes=47 << 20),
            cost_estimate=pl.CostEstimate(flops=0, bytes_accessed=int(3e6 * micros), transcendentals=0),
        )

    panels = [item_factors] + [permute(item_factors, mask) for mask in range(1, panel_total)]
    panel_blocks = panel_rows // block
    item_mask = panel_index * panel_blocks
    own_place = place_of(me ^ (item_mask * (block * device_total // item_rows)), groups)
    entries = (block_user[0] * 256 + (block_item[0] ^ item_mask)) * 256 + jnp.arange(slots, dtype=jnp.int32)
    entries = jnp.concatenate([entries, counts, own_place.astype(jnp.int32).reshape(1)])
    order = pl.pallas_call(
        functools.partial(order_kernel, slots=slots, near_blocks=2 * panel_blocks),
        out_shape=jax.ShapeDtypeStruct((2 * (slots + UNROLL + 16),), jnp.int32),
        in_specs=[SMEM],
        out_specs=SMEM,
        name="order",
        **options(4),
    )(entries)

    sums_shape = jax.ShapeDtypeStruct((item_rows // block, rank, block), jnp.float32)
    user_shape = jax.ShapeDtypeStruct((user_rows, rank), jnp.float32)
    tiles = pltpu.VMEM((slots, block, block), jnp.bfloat16)
    sems = pltpu.SemaphoreType.DMA((turns,))
    whole = pltpu.VMEM((item_rows, rank), jnp.bfloat16)
    near_sums, near_users, turned = pl.pallas_call(
        near_kernel,
        out_shape=(sums_shape, user_shape, jax.ShapeDtypeStruct((user_rows // block, rank, block), jnp.bfloat16)),
        in_specs=[SMEM] + [VMEM] * 3 + [HBM] * 2,
        out_specs=(VMEM,) * 3,
        scratch_shapes=[tiles, tiles, pltpu.VMEM((2 * panel_rows, rank), jnp.bfloat16), sems, sems],
        name="near_sums",
        **options(8),
    )(order, user_factors, panels[0], panels[1], ratings, weights)

    half_shape = jax.ShapeDtypeStruct((item_rows // 2, rank), jnp.float32)
    keep, send, weighted = pl.pallas_call(
        functools.partial(far_kernel, device_total, groups),
        out_shape=(half_shape, half_shape, jax.ShapeDtypeStruct((slots, block, block), jnp.bfloat16)),
        in_specs=[SMEM] + [VMEM] * 3 + [HBM] * 2 + [VMEM] * panel_total,
        out_specs=(VMEM, VMEM, HBM),
        scratch_shapes=[tiles, tiles, whole, pltpu.VMEM(sums_shape.shape, jnp.float32), tiles, sems, sems, sems],
        name="far_sums",
        **options(5),
    )(order, user_factors, turned, near_sums, ratings, weights, *panels)

    partial = keep + permute(send, 1)
    user_grad, token = pl.pallas_call(
        user_kernel,
        out_shape=(user_shape, jax.ShapeDtypeStruct((8, 128), jnp.float32)),
        in_specs=[SMEM] + [VMEM] * 2 + [HBM] + [VMEM] * panel_total,
        out_specs=(HBM, VMEM),
        scratch_shapes=[tiles, whole, pltpu.VMEM(user_shape.shape, user_shape.dtype), sems,
                        pltpu.SemaphoreType.DMA((user_rows // block,))],
        name="user_sums",
        **options(4),
    )(order, user_factors, near_users, weighted, *panels)
    for group in groups[1:]:
        ways = 1 << len(group)
        parts = partial.reshape(ways, -1, rank)
        partial = parts[0]
        for way in reversed(range(1, ways)):
            mask = sum(((way >> index) & 1) << bit for index, bit in enumerate(group))
            partial = partial + permute(parts[way], mask)
        if group is groups[1]:
            partial, token = lax.optimization_barrier((partial, token))
    owned_rows = partial.shape[0]
    first_row = me * owned_rows
    chosen = (first_row // panel_rows) ^ panel_index
    pieces = [lax.dynamic_slice_in_dim(panel, first_row % panel_rows, owned_rows, 0) for panel in panels]
    own_factors = pieces[0]
    for index in range(1, panel_total):
        own_factors = jnp.where(chosen == index, pieces[index], own_factors)
    item_grad = partial * grad_scale + decay_rate * own_factors.astype(jnp.float32)
    return (user_grad, item_grad)


def solution(mesh):
    in_specs = (
        P(AXES, None),
        P("items", None),
        P(AXES, None),
        P(AXES, None),
        P(AXES),
        P(AXES, None, None, None),
        P(AXES, None, None, None),
    )
    out_specs = (P(AXES, None), P(AXES, None))
    return jax.shard_map(body, mesh=mesh, in_specs=in_specs, out_specs=out_specs, check_vma=False)
```

```python
import functools

import jax
import jax.numpy as jnp
from jax import lax
from jax.experimental import pallas as pl
from jax.experimental.pallas import tpu as pltpu
from jax.sharding import PartitionSpec as P

grad_scale = 0.015625
decay_rate = 0.05
AXES = ("users", "items")
UNROLL = 16
VMEM = pl.BlockSpec(memory_space=pltpu.VMEM)
SMEM = pl.BlockSpec(memory_space=pltpu.SMEM)
HBM = pl.BlockSpec(memory_space=pltpu.HBM)


def phases_of(device_total):
    bit_total = device_total.bit_length() - 1
    groups = [[0]]
    for bit in range(1, bit_total, 2):
        groups.append(list(range(bit, min(bit + 2, bit_total))))
    return groups


def place_of(index, groups):
    place = 0
    for group in groups:
        for bit in reversed(group):
            place = place * 2 + ((index >> bit) & 1)
    return place


def stage_kernel(count_ref, user_ref, rating_ref, weight_ref, factor_ref, turned_ref, held_rating_ref, held_weight_ref,
                 factor_sem, rating_sems, weight_sems):
    slots, block = held_rating_ref.shape[0], held_rating_ref.shape[1]
    chunks = (count_ref[0] + UNROLL - 1) // UNROLL

    def copies(index):
        part = pl.ds(index * UNROLL, UNROLL)
        return (
            pltpu.make_async_copy(rating_ref.at[0, part], held_rating_ref.at[part], rating_sems.at[index]),
            pltpu.make_async_copy(weight_ref.at[0, part], held_weight_ref.at[part], weight_sems.at[index]),
        )

    factor_copy = pltpu.make_async_copy(user_ref, factor_ref, factor_sem)
    factor_copy.start()
    for index in range(slots // UNROLL):
        @pl.when(index < chunks)
        def _():
            for copy in copies(index):
                copy.start()
    factor_copy.wait()
    for index in range(turned_ref.shape[0]):
        turned_ref[index] = factor_ref[index * block:(index + 1) * block, :].T
    for index in range(slots // UNROLL):
        @pl.when(index < chunks)
        def _():
            for copy in copies(index):
                copy.wait()


def panel_copies(item_ref, spill_ref, slots, block, sem, out):
    copies = []
    for item in range(item_ref.shape[0] // block):
        for column in range(item_ref.shape[1] // block):
            here = item_ref.at[pl.ds(item * block, block), pl.ds(column * block, block)]
            there = spill_ref.at[slots + item * (item_ref.shape[1] // block) + column]
            copies.append(pltpu.make_async_copy(*((here, there) if out else (there, here)), sem))
    return copies


def item_kernel(owner_total, groups, count_ref, place_ref, user_id_ref, item_id_ref, user_ref, turned_ref, rating_ref,
                weight_ref, *refs):
    panel_refs, refs = refs[:-8], refs[-8:]
    keep_ref, send_ref, spill_ref, item_ref, total, tile_ref, tile_sems, item_sem = refs
    live = count_ref[0]
    item_mask = place_ref[1]
    slots, block = rating_ref.shape[0], rating_ref.shape[1]
    row = 0
    for panel_ref in panel_refs:
        item_ref[row:row + panel_ref.shape[0], :] = panel_ref[...]
        row += panel_ref.shape[0]
    panel_out = panel_copies(item_ref, spill_ref, slots, block, item_sem, True)
    for copy in panel_out:
        copy.start()
    total[...] = jnp.zeros_like(total)
    turns = (live + UNROLL - 1) // UNROLL

    def copy_of(index):
        part = pl.ds(index * UNROLL, UNROLL)
        return pltpu.make_async_copy(tile_ref.at[part], spill_ref.at[part], tile_sems.at[index])

    def turn(index, carry):
        base = index * UNROLL
        predicted = []
        for step in range(UNROLL):
            user_row = pl.multiple_of(user_id_ref[0, base + step] * block, block)
            item_row = pl.multiple_of((item_id_ref[0, base + step] ^ item_mask) * block, block)
            predicted.append(lax.dot_general(
                user_ref[pl.ds(user_row, block), :], item_ref[pl.ds(item_row, block), :],
                (((1,), (1,)), ((), ())), preferred_element_type=jnp.float32))
        terms = []
        for step in range(UNROLL):
            slot = base + step
            weighted = weight_ref[slot].astype(jnp.float32) * (
                predicted[step] - rating_ref[slot].astype(jnp.float32))
            weighted = jnp.where(slot < live, weighted, 0.0).astype(jnp.bfloat16)
            tile_ref[slot] = weighted
            terms.append(jnp.dot(turned_ref[user_id_ref[0, slot]], weighted, preferred_element_type=jnp.float32))
        copy_of(index).start()
        for step in range(UNROLL):
            total[item_id_ref[0, base + step]] += terms[step]
        return carry

    lax.fori_loop(0, turns, turn, 0)
    own_place = place_ref[0]
    owned = keep_ref.shape[0] * 2 // owner_total
    half = owner_total // 2
    per_block = block // owned
    for item in range(total.shape[0]):
        rows = total[item].T
        for part in range(per_block):
            place = own_place ^ place_of(item * per_block + part, groups)
            piece = rows[part * owned:(part + 1) * owned]
            row = pl.multiple_of((place % half) * owned, owned)

            @pl.when(place < half)
            def _():
                keep_ref[pl.ds(row, owned), :] = piece

            @pl.when(place >= half)
            def _():
                send_ref[pl.ds(row, owned), :] = piece

    def finish(index, carry):
        copy_of(index).wait()
        return carry

    lax.fori_loop(0, turns, finish, 0)
    for copy in panel_out:
        copy.wait()


def user_kernel(count_ref, place_ref, user_id_ref, item_id_ref, user_ref, spill_ref, grad_ref, token_ref, tile_ref,
                item_ref, total_ref, tile_sems, item_sem, sems):
    item_mask = place_ref[1]
    slots, block = tile_ref.shape[0], tile_ref.shape[1]
    turns = (count_ref[0] + UNROLL - 1) // UNROLL
    panel_in = panel_copies(item_ref, spill_ref, slots, block, item_sem, False)
    for copy in panel_in:
        copy.start()

    def copy_of(index):
        part = pl.ds(index * UNROLL, UNROLL)
        return pltpu.make_async_copy(spill_ref.at[part], tile_ref.at[part], tile_sems.at[index])

    def prime(index, carry):
        copy_of(index).start()
        return carry

    lax.fori_loop(0, turns, prime, 0)
    token_ref[...] = jnp.zeros_like(token_ref)
    total_ref[...] = jnp.zeros_like(total_ref)
    for copy in panel_in:
        copy.wait()

    def turn(index, carry):
        copy_of(index).wait()
        base = index * UNROLL
        terms = []
        for step in range(UNROLL):
            item_row = pl.multiple_of((item_id_ref[0, base + step] ^ item_mask) * block, block)
            terms.append(jnp.dot(tile_ref[base + step], item_ref[pl.ds(item_row, block), :],
                                 preferred_element_type=jnp.float32))
        for step in range(UNROLL):
            user_row = pl.multiple_of(user_id_ref[0, base + step] * block, block)
            total_ref[pl.ds(user_row, block), :] += terms[step]
        return carry

    lax.fori_loop(0, turns, turn, 0)

    def writeback(index):
        rows = pl.ds(index * block, block)
        return pltpu.make_async_copy(total_ref.at[rows], grad_ref.at[rows], sems.at[index])

    blocks = total_ref.shape[0] // block
    for index in range(blocks):
        rows = pl.ds(index * block, block)
        total_ref[rows, :] = total_ref[rows, :] * grad_scale + decay_rate * user_ref[rows, :].astype(jnp.float32)
        writeback(index).start()
    for index in range(blocks):
        writeback(index).wait()


def sum_kernel(term_total, token_ref, *refs):
    terms, parts = refs[:term_total], refs[term_total:]
    rows = parts[0].shape[0]
    for index, part in enumerate(parts):
        here = pl.ds(index * rows, rows)
        value = terms[0][here, :]
        for term in terms[1:]:
            value = value + term[here, :]
        part[...] = value.astype(part.dtype)


def sum_parts(terms, ways, token):
    rows, rank = terms[0].shape
    shape = jax.ShapeDtypeStruct((rows // ways, rank), jnp.float32)
    return pl.pallas_call(
        functools.partial(sum_kernel, len(terms)),
        out_shape=(shape,) * ways,
        in_specs=[VMEM] * (1 + len(terms)),
        out_specs=(VMEM,) * ways,
        compiler_params=pltpu.CompilerParams(vmem_limit_bytes=8 << 20),
        name="sum_parts",
    )(token, *terms)


def body(user_factors, item_factors, block_user, block_item, counts, ratings, weights):
    rank = user_factors.shape[1]
    slots, block = ratings.shape[1], ratings.shape[2]
    user_rows = user_factors.shape[0]
    panel_rows = item_factors.shape[0]
    panel_total = lax.axis_size("items")
    device_total = lax.axis_size("users") * panel_total
    panel_index = lax.axis_index("items")
    me = lax.axis_index("users") * panel_total + panel_index
    groups = phases_of(device_total)
    item_rows = panel_rows * panel_total
    turns = slots // UNROLL

    def permute(array, mask):
        return lax.ppermute(array, AXES, [(index, index ^ mask) for index in range(device_total)])

    def options(limit, micros):
        return dict(
            compiler_params=pltpu.CompilerParams(vmem_limit_bytes=limit << 20),
            cost_estimate=pl.CostEstimate(flops=0, bytes_accessed=int(3e6 * micros), transcendentals=0),
        )

    panels = [item_factors] + [permute(item_factors, mask) for mask in range(1, panel_total)]
    places = jnp.stack([place_of(me, groups), panel_index * (panel_rows // block)]).astype(jnp.int32)
    held = jax.ShapeDtypeStruct((slots, block, block), jnp.bfloat16)
    tiles = pltpu.VMEM(held.shape, held.dtype)
    sems = pltpu.SemaphoreType.DMA((turns,))
    whole = pltpu.VMEM((item_rows, rank), jnp.bfloat16)
    factors, turned, held_ratings, held_weights = pl.pallas_call(
        stage_kernel,
        out_shape=(
            jax.ShapeDtypeStruct((user_rows, rank), jnp.bfloat16),
            jax.ShapeDtypeStruct((user_rows // block, rank, block), jnp.bfloat16),
            held,
            held,
        ),
        in_specs=[SMEM] + [HBM] * 3,
        out_specs=(VMEM,) * 4,
        scratch_shapes=[pltpu.SemaphoreType.DMA, sems, sems],
        name="stage",
        **options(41, 6),
    )(counts, user_factors, ratings, weights)

    half_shape = jax.ShapeDtypeStruct((item_rows // 2, rank), jnp.float32)
    keep, send, spill = pl.pallas_call(
        functools.partial(item_kernel, device_total, groups),
        out_shape=(half_shape, half_shape, jax.ShapeDtypeStruct((6 * slots, block, block), jnp.bfloat16)),
        in_specs=[SMEM] * 4 + [VMEM] * (4 + panel_total),
        out_specs=(VMEM, VMEM, HBM),
        scratch_shapes=[whole, pltpu.VMEM((item_rows // block, rank, block), jnp.float32), tiles, sems,
                        pltpu.SemaphoreType.DMA],
        name="item_sums",
        **options(41, 8),
    )(counts, places, block_user, block_item, factors, turned, held_ratings, held_weights, *panels)

    terms = [keep, permute(send, 1)]
    user_grad, user_token = pl.pallas_call(
        user_kernel,
        out_shape=(jax.ShapeDtypeStruct((user_rows, rank), jnp.float32), jax.ShapeDtypeStruct((8, 128), jnp.float32)),
        in_specs=[SMEM] * 4 + [VMEM, HBM],
        out_specs=(HBM, VMEM),
        scratch_shapes=[tiles, whole, pltpu.VMEM((user_rows, rank), jnp.float32), sems, pltpu.SemaphoreType.DMA,
                        pltpu.SemaphoreType.DMA((user_rows // block,))],
        name="user_sums",
        **options(44, 5),
    )(counts, places, block_user, block_item, factors, spill)
    token = jnp.zeros((8, 128), jnp.float32)
    for group in groups[1:]:
        ways = 1 << len(group)
        parts = sum_parts(terms, ways, token)
        token = user_token
        terms = [parts[0]]
        for way in reversed(range(1, ways)):
            mask = sum(((way >> index) & 1) << bit for index, bit in enumerate(group))
            terms.append(permute(parts[way], mask))
    partial = functools.reduce(jnp.add, terms)
    owned_rows = partial.shape[0]
    first_row = me * owned_rows
    chosen = (first_row // panel_rows) ^ panel_index
    pieces = [lax.dynamic_slice_in_dim(panel, first_row % panel_rows, owned_rows, 0) for panel in panels]
    own_factors = pieces[0]
    for index in range(1, panel_total):
        own_factors = jnp.where(chosen == index, pieces[index], own_factors)
    item_grad = partial * grad_scale + decay_rate * own_factors.astype(jnp.float32)
    return (user_grad, item_grad)


def solution(mesh):
    in_specs = (
        P(AXES, None),
        P("items", None),
        P(AXES, None),
        P(AXES, None),
        P(AXES),
        P(AXES, None, None, None),
        P(AXES, None, None, None),
    )
    out_specs = (P(AXES, None), P(AXES, None))
    return jax.shard_map(body, mesh=mesh, in_specs=in_specs, out_specs=out_specs, check_vma=False)
```

```python
import functools

import jax
import jax.numpy as jnp
from jax import lax
from jax.experimental import pallas as pl
from jax.experimental.pallas import tpu as pltpu
from jax.sharding import PartitionSpec as P

grad_scale = 0.015625
decay_rate = 0.05
AXES = ("users", "items")
UNROLL = 16
WIDE = 32
VMEM = pl.BlockSpec(memory_space=pltpu.VMEM)
SMEM = pl.BlockSpec(memory_space=pltpu.SMEM)
HBM = pl.BlockSpec(memory_space=pltpu.HBM)


def phases_of(device_total):
    bit_total = device_total.bit_length() - 1
    groups = [[0]]
    for bit in range(1, bit_total, 2):
        groups.append(list(range(bit, min(bit + 2, bit_total))))
    return groups


def place_of(index, groups):
    place = 0
    for group in groups:
        for bit in reversed(group):
            place = place * 2 + ((index >> bit) & 1)
    return place


def stage_kernel(count_ref, user_ref, rating_ref, weight_ref, factor_ref, turned_ref, held_rating_ref, held_weight_ref,
                 factor_sem, rating_sems, weight_sems):
    slots, block = held_rating_ref.shape[0], held_rating_ref.shape[1]
    chunks = (count_ref[0] + UNROLL - 1) // UNROLL

    def copies(index):
        part = pl.ds(index * UNROLL, UNROLL)
        return (
            pltpu.make_async_copy(rating_ref.at[0, part], held_rating_ref.at[part], rating_sems.at[index]),
            pltpu.make_async_copy(weight_ref.at[0, part], held_weight_ref.at[part], weight_sems.at[index]),
        )

    factor_copy = pltpu.make_async_copy(user_ref, factor_ref, factor_sem)
    factor_copy.start()
    for index in range(slots // UNROLL):
        @pl.when(index < chunks)
        def _():
            for copy in copies(index):
                copy.start()
    factor_copy.wait()
    for index in range(turned_ref.shape[0]):
        turned_ref[index] = factor_ref[index * block:(index + 1) * block, :].T
    for index in range(slots // UNROLL):
        @pl.when(index < chunks)
        def _():
            for copy in copies(index):
                copy.wait()


def item_kernel(owner_total, groups, count_ref, place_ref, user_id_ref, item_id_ref, user_ref, turned_ref, rating_ref,
                weight_ref, *refs):
    panel_refs, refs = refs[:-5], refs[-5:]
    keep_ref, send_ref, tile_ref, item_ref, total = refs
    live = count_ref[0]
    item_mask = place_ref[1]
    slots, block = rating_ref.shape[0], rating_ref.shape[1]
    row = 0
    for panel_ref in panel_refs:
        item_ref[row:row + panel_ref.shape[0], :] = panel_ref[...]
        row += panel_ref.shape[0]
    total[...] = jnp.zeros_like(total)
    turns = (live + WIDE - 1) // WIDE

    def turn(index, carry):
        base = index * WIDE
        predicted = []
        for step in range(WIDE):
            user_row = pl.multiple_of(user_id_ref[0, base + step] * block, block)
            item_row = pl.multiple_of((item_id_ref[0, base + step] ^ item_mask) * block, block)
            predicted.append(lax.dot_general(
                user_ref[pl.ds(user_row, block), :], item_ref[pl.ds(item_row, block), :],
                (((1,), (1,)), ((), ())), preferred_element_type=jnp.float32))
        terms = []
        for step in range(WIDE):
            slot = base + step
            weighted = weight_ref[slot].astype(jnp.float32) * (
                predicted[step] - rating_ref[slot].astype(jnp.float32))
            weighted = jnp.where(slot < live, weighted, 0.0).astype(jnp.bfloat16)
            tile_ref[slot] = weighted
            terms.append(jnp.dot(turned_ref[user_id_ref[0, slot]], weighted, preferred_element_type=jnp.float32))
        for step in range(WIDE):
            total[item_id_ref[0, base + step]] += terms[step]
        return carry

    lax.fori_loop(0, turns, turn, 0)
    own_place = place_ref[0]
    owned = keep_ref.shape[0] * 2 // owner_total
    half = owner_total // 2
    per_block = block // owned
    for item in range(total.shape[0]):
        rows = total[item].T
        for part in range(per_block):
            place = own_place ^ place_of(item * per_block + part, groups)
            piece = rows[part * owned:(part + 1) * owned]
            row = pl.multiple_of((place % half) * owned, owned)

            @pl.when(place < half)
            def _():
                keep_ref[pl.ds(row, owned), :] = piece

            @pl.when(place >= half)
            def _():
                send_ref[pl.ds(row, owned), :] = piece


def user_kernel(count_ref, place_ref, user_id_ref, item_id_ref, user_ref, item_ref, tile_ref, grad_ref, token_ref,
                total_ref, sems):
    item_mask = place_ref[1]
    block = tile_ref.shape[1]
    turns = (count_ref[0] + WIDE - 1) // WIDE
    token_ref[...] = jnp.zeros_like(token_ref)
    total_ref[...] = jnp.zeros_like(total_ref)

    def turn(index, carry):
        base = index * WIDE
        terms = []
        for step in range(WIDE):
            item_row = pl.multiple_of((item_id_ref[0, base + step] ^ item_mask) * block, block)
            terms.append(jnp.dot(tile_ref[base + step], item_ref[pl.ds(item_row, block), :],
                                 preferred_element_type=jnp.float32))
        for step in range(WIDE):
            user_row = pl.multiple_of(user_id_ref[0, base + step] * block, block)
            total_ref[pl.ds(user_row, block), :] += terms[step]
        return carry

    lax.fori_loop(0, turns, turn, 0)

    def writeback(index):
        rows = pl.ds(index * block, block)
        return pltpu.make_async_copy(total_ref.at[rows], grad_ref.at[rows], sems.at[index])

    blocks = total_ref.shape[0] // block
    for index in range(blocks):
        rows = pl.ds(index * block, block)
        total_ref[rows, :] = total_ref[rows, :] * grad_scale + decay_rate * user_ref[rows, :].astype(jnp.float32)
        writeback(index).start()
    for index in range(blocks):
        writeback(index).wait()


def sum_kernel(term_total, token_ref, *refs):
    terms, parts = refs[:term_total], refs[term_total:]
    rows = parts[0].shape[0]
    for index, part in enumerate(parts):
        here = pl.ds(index * rows, rows)
        value = terms[0][here, :]
        for term in terms[1:]:
            value = value + term[here, :]
        part[...] = value.astype(part.dtype)


def sum_parts(terms, ways, token):
    rows, rank = terms[0].shape
    shape = jax.ShapeDtypeStruct((rows // ways, rank), jnp.float32)
    return pl.pallas_call(
        functools.partial(sum_kernel, len(terms)),
        out_shape=(shape,) * ways,
        in_specs=[VMEM] * (1 + len(terms)),
        out_specs=(VMEM,) * ways,
        compiler_params=pltpu.CompilerParams(vmem_limit_bytes=8 << 20),
        name="sum_parts",
    )(token, *terms)


def body(user_factors, item_factors, block_user, block_item, counts, ratings, weights):
    rank = user_factors.shape[1]
    slots, block = ratings.shape[1], ratings.shape[2]
    user_rows = user_factors.shape[0]
    panel_rows = item_factors.shape[0]
    panel_total = lax.axis_size("items")
    device_total = lax.axis_size("users") * panel_total
    panel_index = lax.axis_index("items")
    me = lax.axis_index("users") * panel_total + panel_index
    groups = phases_of(device_total)
    item_rows = panel_rows * panel_total
    turns = slots // UNROLL

    def permute(array, mask):
        return lax.ppermute(array, AXES, [(index, index ^ mask) for index in range(device_total)])

    def options(limit, micros):
        return dict(
            compiler_params=pltpu.CompilerParams(vmem_limit_bytes=limit << 20),
            cost_estimate=pl.CostEstimate(flops=0, bytes_accessed=int(3e6 * micros), transcendentals=0),
        )

    panels = [item_factors] + [permute(item_factors, mask) for mask in range(1, panel_total)]
    places = jnp.stack([place_of(me, groups), panel_index * (panel_rows // block)]).astype(jnp.int32)
    held = jax.ShapeDtypeStruct((slots, block, block), jnp.bfloat16)
    sems = pltpu.SemaphoreType.DMA((turns,))
    factors, turned, held_ratings, held_weights = pl.pallas_call(
        stage_kernel,
        out_shape=(
            jax.ShapeDtypeStruct((user_rows, rank), jnp.bfloat16),
            jax.ShapeDtypeStruct((user_rows // block, rank, block), jnp.bfloat16),
            held,
            held,
        ),
        in_specs=[SMEM] + [HBM] * 3,
        out_specs=(VMEM,) * 4,
        scratch_shapes=[pltpu.SemaphoreType.DMA, sems, sems],
        name="stage",
        **options(41, 6),
    )(counts, user_factors, ratings, weights)

    half_shape = jax.ShapeDtypeStruct((item_rows // 2, rank), jnp.float32)
    keep, send, weighted, item_whole = pl.pallas_call(
        functools.partial(item_kernel, device_total, groups),
        out_shape=(half_shape, half_shape, held, jax.ShapeDtypeStruct((item_rows, rank), jnp.bfloat16)),
        in_specs=[SMEM] * 4 + [VMEM] * (4 + panel_total),
        out_specs=(VMEM,) * 4,
        scratch_shapes=[pltpu.VMEM((item_rows // block, rank, block), jnp.float32)],
        name="item_sums",
        **options(12, 8),
    )(counts, places, block_user, block_item, factors, turned, held_ratings, held_weights, *panels)

    terms = [keep, permute(send, 1)]
    user_grad, user_token = pl.pallas_call(
        user_kernel,
        out_shape=(jax.ShapeDtypeStruct((user_rows, rank), jnp.float32), jax.ShapeDtypeStruct((8, 128), jnp.float32)),
        in_specs=[SMEM] * 4 + [VMEM] * 3,
        out_specs=(HBM, VMEM),
        scratch_shapes=[pltpu.VMEM((user_rows, rank), jnp.float32), pltpu.SemaphoreType.DMA((user_rows // block,))],
        name="user_sums",
        **options(8, 5),
    )(counts, places, block_user, block_item, factors, item_whole, weighted)
    token = jnp.zeros((8, 128), jnp.float32)
    for group in groups[1:]:
        ways = 1 << len(group)
        parts = sum_parts(terms, ways, token)
        token = user_token
        terms = [parts[0]]
        for way in reversed(range(1, ways)):
            mask = sum(((way >> index) & 1) << bit for index, bit in enumerate(group))
            terms.append(permute(parts[way], mask))
    partial = functools.reduce(jnp.add, terms)
    owned_rows = partial.shape[0]
    first_row = me * owned_rows
    chosen = (first_row // panel_rows) ^ panel_index
    pieces = [lax.dynamic_slice_in_dim(panel, first_row % panel_rows, owned_rows, 0) for panel in panels]
    own_factors = pieces[0]
    for index in range(1, panel_total):
        own_factors = jnp.where(chosen == index, pieces[index], own_factors)
    item_grad = partial * grad_scale + decay_rate * own_factors.astype(jnp.float32)
    return (user_grad, item_grad)


def solution(mesh):
    in_specs = (
        P(AXES, None),
        P("items", None),
        P(AXES, None),
        P(AXES, None),
        P(AXES),
        P(AXES, None, None, None),
        P(AXES, None, None, None),
    )
    out_specs = (P(AXES, None), P(AXES, None))
    return jax.shard_map(body, mesh=mesh, in_specs=in_specs, out_specs=out_specs, check_vma=False)
```

```python
import functools

import jax
import jax.numpy as jnp
from jax import lax
from jax.experimental import pallas as pl
from jax.experimental.pallas import tpu as pltpu
from jax.sharding import PartitionSpec as P

grad_scale = 0.015625
decay_rate = 0.05
AXES = ("users", "items")
UNROLL = 16
WIDE = 32
VMEM = pl.BlockSpec(memory_space=pltpu.VMEM)
SMEM = pl.BlockSpec(memory_space=pltpu.SMEM)
HBM = pl.BlockSpec(memory_space=pltpu.HBM)


def phases_of(device_total):
    bit_total = device_total.bit_length() - 1
    groups = [[0]]
    for bit in range(1, bit_total, 2):
        groups.append(list(range(bit, min(bit + 2, bit_total))))
    return groups


def place_of(index, groups):
    place = 0
    for group in groups:
        for bit in reversed(group):
            place = place * 2 + ((index >> bit) & 1)
    return place


def stage_kernel(count_ref, user_ref, rating_ref, weight_ref, factor_ref, turned_ref, held_rating_ref, held_weight_ref,
                 factor_sem, rating_sems, weight_sems):
    slots, block = held_rating_ref.shape[0], held_rating_ref.shape[1]
    chunks = (count_ref[0] + UNROLL - 1) // UNROLL

    def copies(index):
        part = pl.ds(index * UNROLL, UNROLL)
        return (
            pltpu.make_async_copy(rating_ref.at[0, part], held_rating_ref.at[part], rating_sems.at[index]),
            pltpu.make_async_copy(weight_ref.at[0, part], held_weight_ref.at[part], weight_sems.at[index]),
        )

    factor_copy = pltpu.make_async_copy(user_ref, factor_ref, factor_sem)
    factor_copy.start()
    for index in range(slots // UNROLL):
        @pl.when(index < chunks)
        def _():
            for copy in copies(index):
                copy.start()
    factor_copy.wait()
    for index in range(turned_ref.shape[0]):
        turned_ref[index] = factor_ref[index * block:(index + 1) * block, :].T
    for index in range(slots // UNROLL):
        @pl.when(index < chunks)
        def _():
            for copy in copies(index):
                copy.wait()


def item_kernel(owner_total, groups, count_ref, place_ref, user_id_ref, item_id_ref, user_ref, turned_ref, rating_ref,
                weight_ref, *refs):
    panel_refs, refs = refs[:-5], refs[-5:]
    keep_ref, send_ref, tile_ref, item_ref, total = refs
    live = count_ref[0]
    item_mask = place_ref[1]
    slots, block = rating_ref.shape[0], rating_ref.shape[1]
    row = 0
    for panel_ref in panel_refs:
        item_ref[row:row + panel_ref.shape[0], :] = panel_ref[...]
        row += panel_ref.shape[0]
    total[...] = jnp.zeros_like(total)
    turns = (live + WIDE - 1) // WIDE

    def turn(index, carry):
        base = index * WIDE
        predicted = []
        for step in range(WIDE):
            user_row = pl.multiple_of(user_id_ref[0, base + step] * block, block)
            item_row = pl.multiple_of((item_id_ref[0, base + step] ^ item_mask) * block, block)
            predicted.append(lax.dot_general(
                user_ref[pl.ds(user_row, block), :], item_ref[pl.ds(item_row, block), :],
                (((1,), (1,)), ((), ())), preferred_element_type=jnp.float32))
        terms = []
        for step in range(WIDE):
            slot = base + step
            weighted = weight_ref[slot].astype(jnp.float32) * (
                predicted[step] - rating_ref[slot].astype(jnp.float32))
            weighted = jnp.where(slot < live, weighted, 0.0).astype(jnp.bfloat16)
            tile_ref[slot] = weighted
            terms.append(jnp.dot(turned_ref[user_id_ref[0, slot]], weighted, preferred_element_type=jnp.float32))
        for step in range(WIDE):
            total[item_id_ref[0, base + step]] += terms[step]
        return carry

    lax.fori_loop(0, turns, turn, 0)
    own_place = place_ref[0]
    owned = keep_ref.shape[0] * 2 // owner_total
    half = owner_total // 2
    per_block = block // owned
    for item in range(total.shape[0]):
        rows = total[item].T
        for part in range(per_block):
            place = own_place ^ place_of(item * per_block + part, groups)
            piece = rows[part * owned:(part + 1) * owned]
            row = pl.multiple_of((place % half) * owned, owned)

            @pl.when(place < half)
            def _():
                keep_ref[pl.ds(row, owned), :] = piece

            @pl.when(place >= half)
            def _():
                send_ref[pl.ds(row, owned), :] = piece


def user_kernel(count_ref, place_ref, user_id_ref, item_id_ref, user_ref, item_ref, tile_ref, grad_ref, token_ref,
                total_ref, sems):
    item_mask = place_ref[1]
    block = tile_ref.shape[1]
    turns = (count_ref[0] + WIDE - 1) // WIDE
    token_ref[...] = jnp.zeros_like(token_ref)
    total_ref[...] = jnp.zeros_like(total_ref)

    def turn(index, carry):
        base = index * WIDE
        terms = []
        for step in range(WIDE):
            item_row = pl.multiple_of((item_id_ref[0, base + step] ^ item_mask) * block, block)
            terms.append(jnp.dot(tile_ref[base + step], item_ref[pl.ds(item_row, block), :],
                                 preferred_element_type=jnp.float32))
        for step in range(WIDE):
            user_row = pl.multiple_of(user_id_ref[0, base + step] * block, block)
            total_ref[pl.ds(user_row, block), :] += terms[step]
        return carry

    lax.fori_loop(0, turns, turn, 0)

    def writeback(index):
        rows = pl.ds(index * block, block)
        return pltpu.make_async_copy(total_ref.at[rows], grad_ref.at[rows], sems.at[index])

    blocks = total_ref.shape[0] // block
    for index in range(blocks):
        rows = pl.ds(index * block, block)
        total_ref[rows, :] = total_ref[rows, :] * grad_scale + decay_rate * user_ref[rows, :].astype(jnp.float32)
        writeback(index).start()
    for index in range(blocks):
        writeback(index).wait()


def sum_kernel(term_total, token_ref, *refs):
    terms, parts = refs[:term_total], refs[term_total:]
    rows = parts[0].shape[0]
    for index, part in enumerate(parts):
        here = pl.ds(index * rows, rows)
        value = terms[0][here, :]
        for term in terms[1:]:
            value = value + term[here, :].astype(jnp.float32)
        part[...] = value.astype(part.dtype)


def sum_parts(terms, ways, token, sent):
    rows, rank = terms[0].shape
    shapes = [jax.ShapeDtypeStruct((rows // ways, rank), kind) for kind in [jnp.float32] + [sent] * (ways - 1)]
    return pl.pallas_call(
        functools.partial(sum_kernel, len(terms)),
        out_shape=tuple(shapes),
        in_specs=[VMEM] * (1 + len(terms)),
        out_specs=(VMEM,) * ways,
        compiler_params=pltpu.CompilerParams(vmem_limit_bytes=8 << 20),
        name="sum_parts",
    )(token, *terms)


def body(user_factors, item_factors, block_user, block_item, counts, ratings, weights):
    rank = user_factors.shape[1]
    slots, block = ratings.shape[1], ratings.shape[2]
    user_rows = user_factors.shape[0]
    panel_rows = item_factors.shape[0]
    panel_total = lax.axis_size("items")
    device_total = lax.axis_size("users") * panel_total
    panel_index = lax.axis_index("items")
    me = lax.axis_index("users") * panel_total + panel_index
    groups = phases_of(device_total)
    item_rows = panel_rows * panel_total
    turns = slots // UNROLL

    def permute(array, mask):
        return lax.ppermute(array, AXES, [(index, index ^ mask) for index in range(device_total)])

    def options(limit, micros):
        return dict(
            compiler_params=pltpu.CompilerParams(vmem_limit_bytes=limit << 20),
            cost_estimate=pl.CostEstimate(flops=0, bytes_accessed=int(3e6 * micros), transcendentals=0),
        )

    panels = [item_factors] + [permute(item_factors, mask) for mask in range(1, panel_total)]
    places = jnp.stack([place_of(me, groups), panel_index * (panel_rows // block)]).astype(jnp.int32)
    held = jax.ShapeDtypeStruct((slots, block, block), jnp.bfloat16)
    sems = pltpu.SemaphoreType.DMA((turns,))
    factors, turned, held_ratings, held_weights = pl.pallas_call(
        stage_kernel,
        out_shape=(
            jax.ShapeDtypeStruct((user_rows, rank), jnp.bfloat16),
            jax.ShapeDtypeStruct((user_rows // block, rank, block), jnp.bfloat16),
            held,
            held,
        ),
        in_specs=[SMEM] + [HBM] * 3,
        out_specs=(VMEM,) * 4,
        scratch_shapes=[pltpu.SemaphoreType.DMA, sems, sems],
        name="stage",
        **options(41, 6),
    )(counts, user_factors, ratings, weights)

    half_shape = jax.ShapeDtypeStruct((item_rows // 2, rank), jnp.float32)
    keep, send, weighted, item_whole = pl.pallas_call(
        functools.partial(item_kernel, device_total, groups),
        out_shape=(half_shape, half_shape, held, jax.ShapeDtypeStruct((item_rows, rank), jnp.bfloat16)),
        in_specs=[SMEM] * 4 + [VMEM] * (4 + panel_total),
        out_specs=(VMEM,) * 4,
        scratch_shapes=[pltpu.VMEM((item_rows // block, rank, block), jnp.float32)],
        name="item_sums",
        **options(12, 8),
    )(counts, places, block_user, block_item, factors, turned, held_ratings, held_weights, *panels)

    terms = [keep, permute(send, 1)]
    user_grad, user_token = pl.pallas_call(
        user_kernel,
        out_shape=(jax.ShapeDtypeStruct((user_rows, rank), jnp.float32), jax.ShapeDtypeStruct((8, 128), jnp.float32)),
        in_specs=[SMEM] * 4 + [VMEM] * 3,
        out_specs=(HBM, VMEM),
        scratch_shapes=[pltpu.VMEM((user_rows, rank), jnp.float32), pltpu.SemaphoreType.DMA((user_rows // block,))],
        name="user_sums",
        **options(8, 5),
    )(counts, places, block_user, block_item, factors, item_whole, weighted)
    token = jnp.zeros((8, 128), jnp.float32)
    for group in groups[1:]:
        ways = 1 << len(group)
        parts = sum_parts(terms, ways, token, jnp.bfloat16 if group is groups[1] else jnp.float32)
        token = user_token
        terms = [parts[0]]
        for way in reversed(range(1, ways)):
            mask = sum(((way >> index) & 1) << bit for index, bit in enumerate(group))
            terms.append(permute(parts[way], mask))
    partial = functools.reduce(jnp.add, terms)
    owned_rows = partial.shape[0]
    first_row = me * owned_rows
    chosen = (first_row // panel_rows) ^ panel_index
    pieces = [lax.dynamic_slice_in_dim(panel, first_row % panel_rows, owned_rows, 0) for panel in panels]
    own_factors = pieces[0]
    for index in range(1, panel_total):
        own_factors = jnp.where(chosen == index, pieces[index], own_factors)
    item_grad = partial * grad_scale + decay_rate * own_factors.astype(jnp.float32)
    return (user_grad, item_grad)


def solution(mesh):
    in_specs = (
        P(AXES, None),
        P("items", None),
        P(AXES, None),
        P(AXES, None),
        P(AXES),
        P(AXES, None, None, None),
        P(AXES, None, None, None),
    )
    out_specs = (P(AXES, None), P(AXES, None))
    return jax.shard_map(body, mesh=mesh, in_specs=in_specs, out_specs=out_specs, check_vma=False)
```

```python
import functools

import jax
import jax.numpy as jnp
from jax import lax
from jax.experimental import pallas as pl
from jax.experimental.pallas import tpu as pltpu
from jax.sharding import PartitionSpec as P

grad_scale = 0.015625
decay_rate = 0.05
AXES = ("users", "items")
UNROLL = 16
WIDE = 32
VMEM = pl.BlockSpec(memory_space=pltpu.VMEM)
SMEM = pl.BlockSpec(memory_space=pltpu.SMEM)
HBM = pl.BlockSpec(memory_space=pltpu.HBM)


def phases_of(device_total):
    bit_total = device_total.bit_length() - 1
    groups = [[0]]
    for bit in range(1, bit_total, 2):
        groups.append(list(range(bit, min(bit + 2, bit_total))))
    return groups


def place_of(index, groups):
    place = 0
    for group in groups:
        for bit in reversed(group):
            place = place * 2 + ((index >> bit) & 1)
    return place


def stage_kernel(count_ref, user_ref, rating_ref, weight_ref, factor_ref, turned_ref, held_rating_ref, held_weight_ref,
                 factor_sem, rating_sems, weight_sems):
    slots, block = held_rating_ref.shape[0], held_rating_ref.shape[1]
    chunks = (count_ref[0] + UNROLL - 1) // UNROLL

    def copies(index):
        part = pl.ds(index * UNROLL, UNROLL)
        return (
            pltpu.make_async_copy(rating_ref.at[0, part], held_rating_ref.at[part], rating_sems.at[index]),
            pltpu.make_async_copy(weight_ref.at[0, part], held_weight_ref.at[part], weight_sems.at[index]),
        )

    factor_copy = pltpu.make_async_copy(user_ref, factor_ref, factor_sem)
    factor_copy.start()
    for index in range(slots // UNROLL):
        @pl.when(index < chunks)
        def _():
            for copy in copies(index):
                copy.start()
    factor_copy.wait()
    for index in range(turned_ref.shape[0]):
        turned_ref[index] = factor_ref[index * block:(index + 1) * block, :].T
    for index in range(slots // UNROLL):
        @pl.when(index < chunks)
        def _():
            for copy in copies(index):
                copy.wait()


def item_kernel(owner_total, groups, count_ref, place_ref, user_id_ref, item_id_ref, user_ref, turned_ref, rating_ref,
                weight_ref, *refs):
    panel_refs, refs = refs[:-5], refs[-5:]
    keep_ref, send_ref, tile_ref, item_ref, total = refs
    live = count_ref[0]
    item_mask = place_ref[1]
    slots, block = rating_ref.shape[0], rating_ref.shape[1]
    row = 0
    for panel_ref in panel_refs:
        item_ref[row:row + panel_ref.shape[0], :] = panel_ref[...]
        row += panel_ref.shape[0]
    total[...] = jnp.zeros_like(total)
    turns = (live + WIDE - 1) // WIDE

    def turn(index, carry):
        base = index * WIDE
        predicted = []
        for step in range(WIDE):
            user_row = pl.multiple_of(user_id_ref[0, base + step] * block, block)
            item_row = pl.multiple_of((item_id_ref[0, base + step] ^ item_mask) * block, block)
            predicted.append(lax.dot_general(
                user_ref[pl.ds(user_row, block), :], item_ref[pl.ds(item_row, block), :],
                (((1,), (1,)), ((), ())), preferred_element_type=jnp.float32))
        terms = []
        for step in range(WIDE):
            slot = base + step
            weighted = weight_ref[slot].astype(jnp.float32) * (
                predicted[step] - rating_ref[slot].astype(jnp.float32))
            weighted = jnp.where(slot < live, weighted, 0.0).astype(jnp.bfloat16)
            tile_ref[slot] = weighted
            terms.append(jnp.dot(turned_ref[user_id_ref[0, slot]], weighted, preferred_element_type=jnp.float32))
        for step in range(WIDE):
            total[item_id_ref[0, base + step]] += terms[step]
        return carry

    lax.fori_loop(0, turns, turn, 0)
    own_place = place_ref[0]
    owned = keep_ref.shape[0] * 2 // owner_total
    half = owner_total // 2
    per_block = block // owned
    for item in range(total.shape[0]):
        rows = total[item].T
        for part in range(per_block):
            place = own_place ^ place_of(item * per_block + part, groups)
            piece = rows[part * owned:(part + 1) * owned]
            row = pl.multiple_of((place % half) * owned, owned)

            @pl.when(place < half)
            def _():
                keep_ref[pl.ds(row, owned), :] = piece

            @pl.when(place >= half)
            def _():
                send_ref[pl.ds(row, owned), :] = piece


def user_kernel(count_ref, place_ref, user_id_ref, item_id_ref, item_ref, tile_ref, total_ref, token_ref):
    item_mask = place_ref[1]
    block = tile_ref.shape[1]
    turns = (count_ref[0] + WIDE - 1) // WIDE
    token_ref[...] = jnp.zeros_like(token_ref)
    total_ref[...] = jnp.zeros_like(total_ref)

    def turn(index, carry):
        base = index * WIDE
        terms = []
        for step in range(WIDE):
            item_row = pl.multiple_of((item_id_ref[0, base + step] ^ item_mask) * block, block)
            terms.append(jnp.dot(tile_ref[base + step], item_ref[pl.ds(item_row, block), :],
                                 preferred_element_type=jnp.float32))
        for step in range(WIDE):
            user_row = pl.multiple_of(user_id_ref[0, base + step] * block, block)
            total_ref[pl.ds(user_row, block), :] += terms[step]
        return carry

    lax.fori_loop(0, turns, turn, 0)


def sum_kernel(term_total, token_ref, *refs):
    terms, parts = refs[:term_total], refs[term_total:]
    rows = parts[0].shape[0]
    for index, part in enumerate(parts):
        here = pl.ds(index * rows, rows)
        value = terms[0][here, :]
        for term in terms[1:]:
            value = value + term[here, :].astype(jnp.float32)
        part[...] = value.astype(part.dtype)


def sum_parts(terms, ways, token, sent):
    rows, rank = terms[0].shape
    shapes = [jax.ShapeDtypeStruct((rows // ways, rank), kind) for kind in [jnp.float32] + [sent] * (ways - 1)]
    return pl.pallas_call(
        functools.partial(sum_kernel, len(terms)),
        out_shape=tuple(shapes),
        in_specs=[VMEM] * (1 + len(terms)),
        out_specs=(VMEM,) * ways,
        compiler_params=pltpu.CompilerParams(vmem_limit_bytes=8 << 20),
        name="sum_parts",
    )(token, *terms)


def body(user_factors, item_factors, block_user, block_item, counts, ratings, weights):
    rank = user_factors.shape[1]
    slots, block = ratings.shape[1], ratings.shape[2]
    user_rows = user_factors.shape[0]
    panel_rows = item_factors.shape[0]
    panel_total = lax.axis_size("items")
    device_total = lax.axis_size("users") * panel_total
    panel_index = lax.axis_index("items")
    me = lax.axis_index("users") * panel_total + panel_index
    groups = phases_of(device_total)
    item_rows = panel_rows * panel_total
    turns = slots // UNROLL

    def permute(array, mask):
        return lax.ppermute(array, AXES, [(index, index ^ mask) for index in range(device_total)])

    def options(limit, micros):
        return dict(
            compiler_params=pltpu.CompilerParams(vmem_limit_bytes=limit << 20),
            cost_estimate=pl.CostEstimate(flops=0, bytes_accessed=int(3e6 * micros), transcendentals=0),
        )

    panels = [item_factors] + [permute(item_factors, mask) for mask in range(1, panel_total)]
    places = jnp.stack([place_of(me, groups), panel_index * (panel_rows // block)]).astype(jnp.int32)
    held = jax.ShapeDtypeStruct((slots, block, block), jnp.bfloat16)
    sems = pltpu.SemaphoreType.DMA((turns,))
    factors, turned, held_ratings, held_weights = pl.pallas_call(
        stage_kernel,
        out_shape=(
            jax.ShapeDtypeStruct((user_rows, rank), jnp.bfloat16),
            jax.ShapeDtypeStruct((user_rows // block, rank, block), jnp.bfloat16),
            held,
            held,
        ),
        in_specs=[SMEM] + [HBM] * 3,
        out_specs=(VMEM,) * 4,
        scratch_shapes=[pltpu.SemaphoreType.DMA, sems, sems],
        name="stage",
        **options(41, 6),
    )(counts, user_factors, ratings, weights)

    half_shape = jax.ShapeDtypeStruct((item_rows // 2, rank), jnp.float32)
    keep, send, weighted, item_whole = pl.pallas_call(
        functools.partial(item_kernel, device_total, groups),
        out_shape=(half_shape, half_shape, held, jax.ShapeDtypeStruct((item_rows, rank), jnp.bfloat16)),
        in_specs=[SMEM] * 4 + [VMEM] * (4 + panel_total),
        out_specs=(VMEM,) * 4,
        scratch_shapes=[pltpu.VMEM((item_rows // block, rank, block), jnp.float32)],
        name="item_sums",
        **options(12, 8),
    )(counts, places, block_user, block_item, factors, turned, held_ratings, held_weights, *panels)

    terms = [keep, permute(send, 1)]
    user_sums, user_token = pl.pallas_call(
        user_kernel,
        out_shape=(jax.ShapeDtypeStruct((user_rows, rank), jnp.float32), jax.ShapeDtypeStruct((8, 128), jnp.float32)),
        in_specs=[SMEM] * 4 + [VMEM] * 2,
        out_specs=(VMEM, VMEM),
        name="user_sums",
        **options(8, 5),
    )(counts, places, block_user, block_item, item_whole, weighted)
    token = jnp.zeros((8, 128), jnp.float32)
    for group in groups[1:]:
        ways = 1 << len(group)
        parts = sum_parts(terms, ways, token, jnp.bfloat16 if group is groups[1] else jnp.float32)
        token = user_token
        kept, late = lax.optimization_barrier((parts[0], me))
        terms = [kept]
        for way in reversed(range(1, ways)):
            mask = sum(((way >> index) & 1) << bit for index, bit in enumerate(group))
            terms.append(permute(parts[way], mask))
    partial = functools.reduce(jnp.add, terms)
    user_grad = user_sums * grad_scale + decay_rate * factors.astype(jnp.float32)
    owned_rows = partial.shape[0]
    first_row = late * owned_rows
    chosen = lax.div(first_row, panel_rows) ^ lax.rem(late, panel_total)
    pieces = [lax.dynamic_slice_in_dim(panel, lax.rem(first_row, panel_rows), owned_rows, 0) for panel in panels]
    own_factors = pieces[0]
    for index in range(1, panel_total):
        own_factors = jnp.where(chosen == index, pieces[index], own_factors)
    item_grad = partial * grad_scale + decay_rate * own_factors.astype(jnp.float32)
    return (user_grad, item_grad)


def solution(mesh):
    in_specs = (
        P(AXES, None),
        P("items", None),
        P(AXES, None),
        P(AXES, None),
        P(AXES),
        P(AXES, None, None, None),
        P(AXES, None, None, None),
    )
    out_specs = (P(AXES, None), P(AXES, None))
    return jax.shard_map(body, mesh=mesh, in_specs=in_specs, out_specs=out_specs, check_vma=False)
```

```python
import functools

import jax
import jax.numpy as jnp
from jax import lax
from jax.experimental import pallas as pl
from jax.experimental.pallas import tpu as pltpu
from jax.sharding import PartitionSpec as P

grad_scale = 0.015625
decay_rate = 0.05
AXES = ("users", "items")
UNROLL = 16
WIDE = 32
VMEM = pl.BlockSpec(memory_space=pltpu.VMEM)
SMEM = pl.BlockSpec(memory_space=pltpu.SMEM)
HBM = pl.BlockSpec(memory_space=pltpu.HBM)


def phases_of(device_total):
    bit_total = device_total.bit_length() - 1
    groups = [[0]]
    for bit in range(1, bit_total, 2):
        groups.append(list(range(bit, min(bit + 2, bit_total))))
    return groups


def place_of(index, groups):
    place = 0
    for group in groups:
        for bit in reversed(group):
            place = place * 2 + ((index >> bit) & 1)
    return place


def stage_kernel(count_ref, place_ref, rating_ref, weight_ref, held_rating_ref, held_weight_ref, token_ref, rating_sems,
                 weight_sems):
    slots = held_rating_ref.shape[0]
    chunks = (count_ref[0] + UNROLL - 1) // UNROLL

    def copies(index):
        part = pl.ds(index * UNROLL, UNROLL)
        return (
            pltpu.make_async_copy(rating_ref.at[0, part], held_rating_ref.at[part], rating_sems.at[index]),
            pltpu.make_async_copy(weight_ref.at[0, part], held_weight_ref.at[part], weight_sems.at[index]),
        )

    for index in range(slots // UNROLL):
        @pl.when(index < chunks)
        def _():
            for copy in copies(index):
                copy.start()
    token_ref[...] = jnp.zeros_like(token_ref) + place_ref[0].astype(jnp.float32)
    for index in range(slots // UNROLL):
        @pl.when(index < chunks)
        def _():
            for copy in copies(index):
                copy.wait()


def item_kernel(owner_total, groups, count_ref, place_ref, user_id_ref, item_id_ref, user_ref, token_ref, rating_ref,
                weight_ref, *refs):
    panel_refs, refs = refs[:-5], refs[-5:]
    keep_ref, send_ref, tile_ref, item_ref, total = refs
    live = count_ref[0]
    item_mask = place_ref[1]
    slots, block = rating_ref.shape[0], rating_ref.shape[1]
    row = 0
    for panel_ref in panel_refs:
        item_ref[row:row + panel_ref.shape[0], :] = panel_ref[...]
        row += panel_ref.shape[0]
    total[...] = jnp.zeros_like(total)
    turns = (live + WIDE - 1) // WIDE

    def turn(index, carry):
        base = index * WIDE
        predicted = []
        for step in range(WIDE):
            user_row = pl.multiple_of(user_id_ref[0, base + step] * block, block)
            item_row = pl.multiple_of((item_id_ref[0, base + step] ^ item_mask) * block, block)
            predicted.append(lax.dot_general(
                user_ref[pl.ds(user_row, block), :], item_ref[pl.ds(item_row, block), :],
                (((1,), (1,)), ((), ())), preferred_element_type=jnp.float32))
        terms = []
        for step in range(WIDE):
            slot = base + step
            weighted = weight_ref[slot].astype(jnp.float32) * (
                predicted[step] - rating_ref[slot].astype(jnp.float32))
            weighted = jnp.where(slot < live, weighted, 0.0).astype(jnp.bfloat16)
            tile_ref[slot] = weighted
            user_row = pl.multiple_of(user_id_ref[0, slot] * block, block)
            terms.append(lax.dot_general(
                weighted, user_ref[pl.ds(user_row, block), :],
                (((0,), (0,)), ((), ())), preferred_element_type=jnp.float32))
        for step in range(WIDE):
            total[item_id_ref[0, base + step]] += terms[step]
        return carry

    lax.fori_loop(0, turns, turn, 0)
    own_place = place_ref[0]
    owned = keep_ref.shape[0] * 2 // owner_total
    half = owner_total // 2
    per_block = block // owned
    for flip in range(2):
        @pl.when(own_place // half == flip)
        def _():
            for owner in range(owner_total):
                place = place_of(owner, groups)
                target = send_ref if (place // half) ^ flip else keep_ref
                row = pl.multiple_of(((own_place ^ place) % half) * owned, owned)
                part = owner % per_block * owned
                target[pl.ds(row, owned), :] = total[owner // per_block, part:part + owned, :]


def user_kernel(count_ref, place_ref, user_id_ref, item_id_ref, item_ref, tile_ref, total_ref, token_ref):
    item_mask = place_ref[1]
    block = tile_ref.shape[1]
    turns = (count_ref[0] + WIDE - 1) // WIDE
    token_ref[...] = jnp.zeros_like(token_ref)
    total_ref[...] = jnp.zeros_like(total_ref)

    def turn(index, carry):
        base = index * WIDE
        terms = []
        for step in range(WIDE):
            item_row = pl.multiple_of((item_id_ref[0, base + step] ^ item_mask) * block, block)
            terms.append(jnp.dot(tile_ref[base + step], item_ref[pl.ds(item_row, block), :],
                                 preferred_element_type=jnp.float32))
        for step in range(WIDE):
            user_row = pl.multiple_of(user_id_ref[0, base + step] * block, block)
            total_ref[pl.ds(user_row, block), :] += terms[step]
        return carry

    lax.fori_loop(0, turns, turn, 0)


def sum_kernel(term_total, token_ref, *refs):
    terms, parts = refs[:term_total], refs[term_total:]
    rows = parts[0].shape[0]
    for index, part in enumerate(parts):
        here = pl.ds(index * rows, rows)
        value = terms[0][here, :]
        for term in terms[1:]:
            value = value + term[here, :].astype(jnp.float32)
        part[...] = value.astype(part.dtype)


def sum_parts(terms, ways, token, sent):
    rows, rank = terms[0].shape
    shapes = [jax.ShapeDtypeStruct((rows // ways, rank), kind) for kind in [jnp.float32] + [sent] * (ways - 1)]
    return pl.pallas_call(
        functools.partial(sum_kernel, len(terms)),
        out_shape=tuple(shapes),
        in_specs=[VMEM] * (1 + len(terms)),
        out_specs=(VMEM,) * ways,
        compiler_params=pltpu.CompilerParams(vmem_limit_bytes=8 << 20),
        name="sum_parts",
    )(token, *terms)


def body(user_factors, item_factors, block_user, block_item, counts, ratings, weights):
    rank = user_factors.shape[1]
    slots, block = ratings.shape[1], ratings.shape[2]
    user_rows = user_factors.shape[0]
    panel_rows = item_factors.shape[0]
    panel_total = lax.axis_size("items")
    device_total = lax.axis_size("users") * panel_total
    panel_index = lax.axis_index("items")
    me = lax.axis_index("users") * panel_total + panel_index
    groups = phases_of(device_total)
    item_rows = panel_rows * panel_total
    turns = slots // UNROLL

    def permute(array, mask):
        return lax.ppermute(array, AXES, [(index, index ^ mask) for index in range(device_total)])

    def options(limit, micros):
        return dict(
            compiler_params=pltpu.CompilerParams(vmem_limit_bytes=limit << 20),
            cost_estimate=pl.CostEstimate(flops=0, bytes_accessed=int(3e6 * micros), transcendentals=0),
        )

    places = jnp.stack([place_of(me, groups), panel_index * (panel_rows // block)]).astype(jnp.int32)
    held = jax.ShapeDtypeStruct((slots, block, block), jnp.bfloat16)
    sems = pltpu.SemaphoreType.DMA((turns,))
    direct = {mask: permute(item_factors, mask) for mask in [*range(2, panel_total, 2), 1]}
    held_ratings, held_weights, token = pl.pallas_call(
        stage_kernel,
        out_shape=(held, held, jax.ShapeDtypeStruct((8, 128), jnp.float32)),
        in_specs=[SMEM] * 2 + [HBM] * 2,
        out_specs=(VMEM,) * 3,
        scratch_shapes=[sems, sems],
        name="stage",
        **options(44, 6),
    )(counts, places, ratings, weights)
    panels = {0: item_factors, 1: direct[1]}
    for mask in range(2, panel_total, 2):
        panels[mask], token = lax.optimization_barrier((direct[mask], token))
        panels[mask + 1] = permute(panels[mask], 1)
    panels = [panels[mask] for mask in range(panel_total)]

    half_shape = jax.ShapeDtypeStruct((item_rows // 2, rank), jnp.float32)
    keep, send, weighted, item_whole = pl.pallas_call(
        functools.partial(item_kernel, device_total, groups),
        out_shape=(half_shape, half_shape, held, jax.ShapeDtypeStruct((item_rows, rank), jnp.bfloat16)),
        in_specs=[SMEM] * 4 + [VMEM] * (4 + panel_total),
        out_specs=(VMEM,) * 4,
        scratch_shapes=[pltpu.VMEM((item_rows // block, block, rank), jnp.float32)],
        name="item_sums",
        **options(12, 8),
    )(counts, places, block_user, block_item, user_factors, token, held_ratings, held_weights, *panels)

    terms = [keep, permute(send, 1)]
    user_sums, user_token = pl.pallas_call(
        user_kernel,
        out_shape=(jax.ShapeDtypeStruct((user_rows, rank), jnp.float32), jax.ShapeDtypeStruct((8, 128), jnp.float32)),
        in_specs=[SMEM] * 4 + [VMEM] * 2,
        out_specs=(VMEM, VMEM),
        name="user_sums",
        **options(8, 5),
    )(counts, places, block_user, block_item, item_whole, weighted)
    token = jnp.zeros((8, 128), jnp.float32)
    for group in groups[1:]:
        ways = 1 << len(group)
        parts = sum_parts(terms, ways, token, jnp.bfloat16 if group is groups[1] else jnp.float32)
        token = user_token
        kept, late = lax.optimization_barrier((parts[0], me))
        terms = [kept]
        for way in reversed(range(1, ways)):
            mask = sum(((way >> index) & 1) << bit for index, bit in enumerate(group))
            terms.append(permute(parts[way], mask))
    partial = functools.reduce(jnp.add, terms)
    user_grad = user_sums * grad_scale + decay_rate * user_factors.astype(jnp.float32)
    owned_rows = partial.shape[0]
    first_row = late * owned_rows
    chosen = lax.div(first_row, panel_rows) ^ lax.rem(late, panel_total)
    pieces = [lax.dynamic_slice_in_dim(panel, lax.rem(first_row, panel_rows), owned_rows, 0) for panel in panels]
    own_factors = pieces[0]
    for index in range(1, panel_total):
        own_factors = jnp.where(chosen == index, pieces[index], own_factors)
    item_grad = partial * grad_scale + decay_rate * own_factors.astype(jnp.float32)
    return (user_grad, item_grad)


def solution(mesh):
    in_specs = (
        P(AXES, None),
        P("items", None),
        P(AXES, None),
        P(AXES, None),
        P(AXES),
        P(AXES, None, None, None),
        P(AXES, None, None, None),
    )
    out_specs = (P(AXES, None), P(AXES, None))
    return jax.shard_map(body, mesh=mesh, in_specs=in_specs, out_specs=out_specs, check_vma=False)
```

```python
import functools

import jax
import jax.numpy as jnp
from jax import lax
from jax.experimental import pallas as pl
from jax.experimental.pallas import tpu as pltpu
from jax.sharding import PartitionSpec as P

grad_scale = 0.015625
decay_rate = 0.05
AXES = ("users", "items")
UNROLL = 16
WIDE = 32
WIDEST = 64
VMEM = pl.BlockSpec(memory_space=pltpu.VMEM)
SMEM = pl.BlockSpec(memory_space=pltpu.SMEM)
HBM = pl.BlockSpec(memory_space=pltpu.HBM)


def phases_of(device_total):
    bit_total = device_total.bit_length() - 1
    groups = [[0]]
    for bit in range(1, bit_total, 2):
        groups.append(list(range(bit, min(bit + 2, bit_total))))
    return groups


def place_of(index, groups):
    place = 0
    for group in groups:
        for bit in reversed(group):
            place = place * 2 + ((index >> bit) & 1)
    return place


def stage_kernel(count_ref, place_ref, rating_ref, weight_ref, held_rating_ref, held_weight_ref, token_ref, rating_sems,
                 weight_sems):
    slots = held_rating_ref.shape[0]
    chunks = (count_ref[0] + UNROLL - 1) // UNROLL

    def copies(index):
        part = pl.ds(index * UNROLL, UNROLL)
        return (
            pltpu.make_async_copy(rating_ref.at[0, part], held_rating_ref.at[part], rating_sems.at[index]),
            pltpu.make_async_copy(weight_ref.at[0, part], held_weight_ref.at[part], weight_sems.at[index]),
        )

    for index in range(slots // UNROLL):
        @pl.when(index < chunks)
        def _():
            for copy in copies(index):
                copy.start()
    token_ref[...] = jnp.zeros_like(token_ref) + place_ref[0].astype(jnp.float32)
    for index in range(slots // UNROLL):
        @pl.when(index < chunks)
        def _():
            for copy in copies(index):
                copy.wait()


def item_kernel(owner_total, groups, count_ref, place_ref, user_id_ref, item_id_ref, user_ref, token_ref, rating_ref,
                weight_ref, *refs):
    panel_refs, refs = refs[:-5], refs[-5:]
    keep_ref, send_ref, tile_ref, item_ref, total = refs
    live = count_ref[0]
    item_mask = place_ref[1]
    slots, block = rating_ref.shape[0], rating_ref.shape[1]
    row = 0
    for panel_ref in panel_refs:
        item_ref[row:row + panel_ref.shape[0], :] = panel_ref[...]
        row += panel_ref.shape[0]
    total[...] = jnp.zeros_like(total)
    turns = (live + WIDEST - 1) // WIDEST

    def turn(index, carry):
        base = index * WIDEST
        predicted = []
        for step in range(WIDEST):
            user_row = pl.multiple_of(user_id_ref[0, base + step] * block, block)
            item_row = pl.multiple_of((item_id_ref[0, base + step] ^ item_mask) * block, block)
            predicted.append(lax.dot_general(
                user_ref[pl.ds(user_row, block), :], item_ref[pl.ds(item_row, block), :],
                (((1,), (1,)), ((), ())), preferred_element_type=jnp.float32))
        terms = []
        for step in range(WIDEST):
            slot = base + step
            weighted = weight_ref[slot].astype(jnp.float32) * (
                predicted[step] - rating_ref[slot].astype(jnp.float32))
            weighted = jnp.where(slot < live, weighted, 0.0).astype(jnp.bfloat16)
            tile_ref[slot] = weighted
            user_row = pl.multiple_of(user_id_ref[0, slot] * block, block)
            terms.append(lax.dot_general(
                weighted, user_ref[pl.ds(user_row, block), :],
                (((0,), (0,)), ((), ())), preferred_element_type=jnp.float32))
        for step in range(WIDEST):
            total[item_id_ref[0, base + step]] += terms[step]
        return carry

    lax.fori_loop(0, turns, turn, 0)
    own_place = place_ref[0]
    owned = keep_ref.shape[0] * 2 // owner_total
    half = owner_total // 2
    per_block = block // owned
    for flip in range(2):
        @pl.when(own_place // half == flip)
        def _():
            for owner in range(owner_total):
                place = place_of(owner, groups)
                target = send_ref if (place // half) ^ flip else keep_ref
                row = pl.multiple_of(((own_place ^ place) % half) * owned, owned)
                part = owner % per_block * owned
                piece = total[owner // per_block, part:part + owned, :]
                target[pl.ds(row, owned), :] = piece.astype(target.dtype)


def user_kernel(count_ref, place_ref, user_id_ref, item_id_ref, item_ref, tile_ref, total_ref, token_ref):
    item_mask = place_ref[1]
    block = tile_ref.shape[1]
    turns = (count_ref[0] + WIDE - 1) // WIDE
    token_ref[...] = jnp.zeros_like(token_ref)
    total_ref[...] = jnp.zeros_like(total_ref)

    def turn(index, carry):
        base = index * WIDE
        terms = []
        for step in range(WIDE):
            item_row = pl.multiple_of((item_id_ref[0, base + step] ^ item_mask) * block, block)
            terms.append(jnp.dot(tile_ref[base + step], item_ref[pl.ds(item_row, block), :],
                                 preferred_element_type=jnp.float32))
        for step in range(WIDE):
            user_row = pl.multiple_of(user_id_ref[0, base + step] * block, block)
            total_ref[pl.ds(user_row, block), :] += terms[step]
        return carry

    lax.fori_loop(0, turns, turn, 0)


def sum_kernel(term_total, token_ref, *refs):
    terms, parts = refs[:term_total], refs[term_total:]
    rows = parts[0].shape[0]
    for index, part in enumerate(parts):
        here = pl.ds(index * rows, rows)
        value = terms[0][here, :]
        for term in terms[1:]:
            value = value + term[here, :].astype(jnp.float32)
        part[...] = value.astype(part.dtype)


def sum_parts(terms, ways, token, sent):
    rows, rank = terms[0].shape
    shapes = [jax.ShapeDtypeStruct((rows // ways, rank), kind) for kind in [jnp.float32] + [sent] * (ways - 1)]
    return pl.pallas_call(
        functools.partial(sum_kernel, len(terms)),
        out_shape=tuple(shapes),
        in_specs=[VMEM] * (1 + len(terms)),
        out_specs=(VMEM,) * ways,
        compiler_params=pltpu.CompilerParams(vmem_limit_bytes=8 << 20),
        name="sum_parts",
    )(token, *terms)


def body(user_factors, item_factors, block_user, block_item, counts, ratings, weights):
    rank = user_factors.shape[1]
    slots, block = ratings.shape[1], ratings.shape[2]
    user_rows = user_factors.shape[0]
    panel_rows = item_factors.shape[0]
    panel_total = lax.axis_size("items")
    device_total = lax.axis_size("users") * panel_total
    panel_index = lax.axis_index("items")
    me = lax.axis_index("users") * panel_total + panel_index
    groups = phases_of(device_total)
    item_rows = panel_rows * panel_total
    turns = slots // UNROLL

    def permute(array, mask):
        return lax.ppermute(array, AXES, [(index, index ^ mask) for index in range(device_total)])

    def options(limit, micros):
        return dict(
            compiler_params=pltpu.CompilerParams(vmem_limit_bytes=limit << 20),
            cost_estimate=pl.CostEstimate(flops=0, bytes_accessed=int(3e6 * micros), transcendentals=0),
        )

    places = jnp.stack([place_of(me, groups), panel_index * (panel_rows // block)]).astype(jnp.int32)
    held = jax.ShapeDtypeStruct((slots, block, block), jnp.bfloat16)
    sems = pltpu.SemaphoreType.DMA((turns,))
    direct = {mask: permute(item_factors, mask) for mask in [*range(2, panel_total, 2), 1]}
    held_ratings, held_weights, token = pl.pallas_call(
        stage_kernel,
        out_shape=(held, held, jax.ShapeDtypeStruct((8, 128), jnp.float32)),
        in_specs=[SMEM] * 2 + [HBM] * 2,
        out_specs=(VMEM,) * 3,
        scratch_shapes=[sems, sems],
        name="stage",
        **options(44, 6),
    )(counts, places, ratings, weights)
    panels = {0: item_factors, 1: direct[1]}
    for mask in range(2, panel_total, 2):
        panels[mask], token = lax.optimization_barrier((direct[mask], token))
        panels[mask + 1] = permute(panels[mask], 1)
    panels = [panels[mask] for mask in range(panel_total)]

    half_shape = jax.ShapeDtypeStruct((item_rows // 2, rank), jnp.float32)
    narrow = item_rows // device_total % 16 == 0
    sent_shape = jax.ShapeDtypeStruct(half_shape.shape, jnp.bfloat16 if narrow else jnp.float32)
    keep, send, weighted, item_whole = pl.pallas_call(
        functools.partial(item_kernel, device_total, groups),
        out_shape=(half_shape, sent_shape, held, jax.ShapeDtypeStruct((item_rows, rank), jnp.bfloat16)),
        in_specs=[SMEM] * 4 + [VMEM] * (4 + panel_total),
        out_specs=(VMEM,) * 4,
        scratch_shapes=[pltpu.VMEM((item_rows // block, block, rank), jnp.float32)],
        name="item_sums",
        **options(12, 8),
    )(counts, places, block_user, block_item, user_factors, token, held_ratings, held_weights, *panels)

    terms = [keep, permute(send, 1)]
    user_sums, user_token = pl.pallas_call(
        user_kernel,
        out_shape=(jax.ShapeDtypeStruct((user_rows, rank), jnp.float32), jax.ShapeDtypeStruct((8, 128), jnp.float32)),
        in_specs=[SMEM] * 4 + [VMEM] * 2,
        out_specs=(VMEM, VMEM),
        name="user_sums",
        **options(8, 5),
    )(counts, places, block_user, block_item, item_whole, weighted)
    token = jnp.zeros((8, 128), jnp.float32)
    for group in groups[1:]:
        ways = 1 << len(group)
        parts = sum_parts(terms, ways, token, jnp.bfloat16 if group is groups[1] else jnp.float32)
        token = user_token
        kept, late = lax.optimization_barrier((parts[0], me))
        terms = [kept]
        for way in reversed(range(1, ways)):
            mask = sum(((way >> index) & 1) << bit for index, bit in enumerate(group))
            terms.append(permute(parts[way], mask))
    partial = functools.reduce(jnp.add, terms)
    user_grad = user_sums * grad_scale + decay_rate * user_factors.astype(jnp.float32)
    owned_rows = partial.shape[0]
    first_row = late * owned_rows
    chosen = lax.div(first_row, panel_rows) ^ lax.rem(late, panel_total)
    pieces = [lax.dynamic_slice_in_dim(panel, lax.rem(first_row, panel_rows), owned_rows, 0) for panel in panels]
    own_factors = pieces[0]
    for index in range(1, panel_total):
        own_factors = jnp.where(chosen == index, pieces[index], own_factors)
    item_grad = partial * grad_scale + decay_rate * own_factors.astype(jnp.float32)
    return (user_grad, item_grad)


def solution(mesh):
    in_specs = (
        P(AXES, None),
        P("items", None),
        P(AXES, None),
        P(AXES, None),
        P(AXES),
        P(AXES, None, None, None),
        P(AXES, None, None, None),
    )
    out_specs = (P(AXES, None), P(AXES, None))
    return jax.shard_map(body, mesh=mesh, in_specs=in_specs, out_specs=out_specs, check_vma=False)
```

```python
import functools

import jax
import jax.numpy as jnp
from jax import lax
from jax.experimental import pallas as pl
from jax.experimental.pallas import tpu as pltpu
from jax.sharding import PartitionSpec as P

grad_scale = 0.015625
decay_rate = 0.05
AXES = ("users", "items")
UNROLL = 16
WIDE = 32
WIDEST = 64
VMEM = pl.BlockSpec(memory_space=pltpu.VMEM)
SMEM = pl.BlockSpec(memory_space=pltpu.SMEM)
HBM = pl.BlockSpec(memory_space=pltpu.HBM)


def phases_of(device_total):
    bit_total = device_total.bit_length() - 1
    groups = [[0]]
    for bit in range(1, bit_total, 2):
        groups.append(list(range(bit, min(bit + 2, bit_total))))
    return groups


def place_of(index, groups):
    place = 0
    for group in groups:
        for bit in reversed(group):
            place = place * 2 + ((index >> bit) & 1)
    return place


def stage_kernel(count_ref, place_ref, rating_ref, weight_ref, held_rating_ref, held_weight_ref, token_ref, rating_sems,
                 weight_sems):
    slots = held_rating_ref.shape[0]
    chunks = (count_ref[0] + UNROLL - 1) // UNROLL

    def copies(index):
        part = pl.ds(index * UNROLL, UNROLL)
        return (
            pltpu.make_async_copy(rating_ref.at[0, part], held_rating_ref.at[part], rating_sems.at[index]),
            pltpu.make_async_copy(weight_ref.at[0, part], held_weight_ref.at[part], weight_sems.at[index]),
        )

    for index in range(slots // UNROLL):
        @pl.when(index < chunks)
        def _():
            for copy in copies(index):
                copy.start()
    token_ref[...] = jnp.zeros_like(token_ref) + place_ref[0].astype(jnp.float32)
    for index in range(slots // UNROLL):
        @pl.when(index < chunks)
        def _():
            for copy in copies(index):
                copy.wait()


def item_kernel(owner_total, groups, count_ref, place_ref, user_id_ref, item_id_ref, user_ref, token_ref, rating_ref,
                weight_ref, *refs):
    panel_refs, refs = refs[:-5], refs[-5:]
    keep_ref, send_ref, tile_ref, item_ref, total = refs
    live = count_ref[0]
    item_mask = place_ref[1]
    slots, block = rating_ref.shape[0], rating_ref.shape[1]
    row = 0
    for panel_ref in panel_refs:
        item_ref[row:row + panel_ref.shape[0], :] = panel_ref[...]
        row += panel_ref.shape[0]
    total[...] = jnp.zeros_like(total)
    turns = (live + WIDEST - 1) // WIDEST

    def turn(index, carry):
        base = index * WIDEST
        predicted = []
        for step in range(WIDEST):
            user_row = pl.multiple_of(user_id_ref[0, base + step] * block, block)
            item_row = pl.multiple_of((item_id_ref[0, base + step] ^ item_mask) * block, block)
            predicted.append(lax.dot_general(
                user_ref[pl.ds(user_row, block), :], item_ref[pl.ds(item_row, block), :],
                (((1,), (1,)), ((), ())), preferred_element_type=jnp.float32))
        terms = []
        for step in range(WIDEST):
            slot = base + step
            weighted = weight_ref[slot].astype(jnp.float32) * (
                predicted[step] - rating_ref[slot].astype(jnp.float32))
            weighted = jnp.where(slot < live, weighted, 0.0).astype(jnp.bfloat16)
            tile_ref[slot] = weighted
            user_row = pl.multiple_of(user_id_ref[0, slot] * block, block)
            terms.append(lax.dot_general(
                weighted, user_ref[pl.ds(user_row, block), :],
                (((0,), (0,)), ((), ())), preferred_element_type=jnp.float32))
        for step in range(WIDEST):
            total[item_id_ref[0, base + step]] += terms[step]
        return carry

    lax.fori_loop(0, turns, turn, 0)
    own_place = place_of(place_ref[0], groups)
    owned = keep_ref.shape[0] * 2 // owner_total
    half = owner_total // 2
    per_block = block // owned
    for flip in range(2):
        @pl.when(own_place // half == flip)
        def _():
            for owner in range(owner_total):
                place = place_of(owner, groups)
                target = send_ref if (place // half) ^ flip else keep_ref
                row = pl.multiple_of(((own_place ^ place) % half) * owned, owned)
                part = owner % per_block * owned
                piece = total[owner // per_block, part:part + owned, :]
                target[pl.ds(row, owned), :] = piece.astype(target.dtype)


def user_kernel(count_ref, place_ref, user_id_ref, item_id_ref, item_ref, tile_ref, total_ref, token_ref):
    item_mask = place_ref[1]
    block = tile_ref.shape[1]
    turns = (count_ref[0] + WIDE - 1) // WIDE
    token_ref[...] = jnp.zeros_like(token_ref)
    total_ref[...] = jnp.zeros_like(total_ref)

    def turn(index, carry):
        base = index * WIDE
        terms = []
        for step in range(WIDE):
            item_row = pl.multiple_of((item_id_ref[0, base + step] ^ item_mask) * block, block)
            terms.append(jnp.dot(tile_ref[base + step], item_ref[pl.ds(item_row, block), :],
                                 preferred_element_type=jnp.float32))
        for step in range(WIDE):
            user_row = pl.multiple_of(user_id_ref[0, base + step] * block, block)
            total_ref[pl.ds(user_row, block), :] += terms[step]
        return carry

    lax.fori_loop(0, turns, turn, 0)


def sum_kernel(term_total, token_ref, *refs):
    terms, parts = refs[:term_total], refs[term_total:]
    rows = parts[0].shape[0]
    for index, part in enumerate(parts):
        here = pl.ds(index * rows, rows)
        value = terms[0][here, :]
        for term in terms[1:]:
            value = value + term[here, :].astype(jnp.float32)
        part[...] = value.astype(part.dtype)


def sum_parts(terms, ways, token, sent):
    rows, rank = terms[0].shape
    shapes = [jax.ShapeDtypeStruct((rows // ways, rank), kind) for kind in [jnp.float32] + [sent] * (ways - 1)]
    return pl.pallas_call(
        functools.partial(sum_kernel, len(terms)),
        out_shape=tuple(shapes),
        in_specs=[VMEM] * (1 + len(terms)),
        out_specs=(VMEM,) * ways,
        compiler_params=pltpu.CompilerParams(vmem_limit_bytes=8 << 20),
        name="sum_parts",
    )(token, *terms)


def body(user_factors, item_factors, block_user, block_item, counts, ratings, weights):
    rank = user_factors.shape[1]
    slots, block = ratings.shape[1], ratings.shape[2]
    user_rows = user_factors.shape[0]
    panel_rows = item_factors.shape[0]
    panel_total = lax.axis_size("items")
    device_total = lax.axis_size("users") * panel_total
    panel_index = lax.axis_index("items")
    me = lax.axis_index("users") * panel_total + panel_index
    groups = phases_of(device_total)
    item_rows = panel_rows * panel_total
    turns = slots // UNROLL

    def permute(array, mask):
        return lax.ppermute(array, AXES, [(index, index ^ mask) for index in range(device_total)])

    def options(limit, micros):
        return dict(
            compiler_params=pltpu.CompilerParams(vmem_limit_bytes=limit << 20),
            cost_estimate=pl.CostEstimate(flops=0, bytes_accessed=int(3e6 * micros), transcendentals=0),
        )

    places = jnp.stack([me, panel_index * (panel_rows // block)]).astype(jnp.int32)
    held = jax.ShapeDtypeStruct((slots, block, block), jnp.bfloat16)
    sems = pltpu.SemaphoreType.DMA((turns,))
    direct = {mask: permute(item_factors, mask) for mask in [*range(2, panel_total, 2), 1]}
    held_ratings, held_weights, token = pl.pallas_call(
        stage_kernel,
        out_shape=(held, held, jax.ShapeDtypeStruct((8, 128), jnp.float32)),
        in_specs=[SMEM] * 2 + [HBM] * 2,
        out_specs=(VMEM,) * 3,
        scratch_shapes=[sems, sems],
        name="stage",
        **options(44, 6),
    )(counts, places, ratings, weights)
    panels = {0: item_factors, 1: direct[1]}
    for mask in range(2, panel_total, 2):
        panels[mask], token = lax.optimization_barrier((direct[mask], token))
        panels[mask + 1] = permute(panels[mask], 1)
    panels = [panels[mask] for mask in range(panel_total)]

    half_shape = jax.ShapeDtypeStruct((item_rows // 2, rank), jnp.float32)
    narrow = item_rows // device_total % 16 == 0
    sent_shape = jax.ShapeDtypeStruct(half_shape.shape, jnp.bfloat16 if narrow else jnp.float32)
    keep, send, weighted, item_whole = pl.pallas_call(
        functools.partial(item_kernel, device_total, groups),
        out_shape=(half_shape, sent_shape, held, jax.ShapeDtypeStruct((item_rows, rank), jnp.bfloat16)),
        in_specs=[SMEM] * 4 + [VMEM] * (4 + panel_total),
        out_specs=(VMEM,) * 4,
        scratch_shapes=[pltpu.VMEM((item_rows // block, block, rank), jnp.float32)],
        name="item_sums",
        **options(12, 8),
    )(counts, places, block_user, block_item, user_factors, token, held_ratings, held_weights, *panels)

    terms = [keep, permute(send, 1)]
    user_sums, user_token = pl.pallas_call(
        user_kernel,
        out_shape=(jax.ShapeDtypeStruct((user_rows, rank), jnp.float32), jax.ShapeDtypeStruct((8, 128), jnp.float32)),
        in_specs=[SMEM] * 4 + [VMEM] * 2,
        out_specs=(VMEM, VMEM),
        name="user_sums",
        **options(8, 5),
    )(counts, places, block_user, block_item, item_whole, weighted)
    token = jnp.zeros((8, 128), jnp.float32)
    for group in groups[1:]:
        ways = 1 << len(group)
        parts = sum_parts(terms, ways, token, jnp.bfloat16 if group is groups[1] else jnp.float32)
        token = user_token
        kept, late = lax.optimization_barrier((parts[0], me))
        terms = [kept]
        for way in reversed(range(1, ways)):
            mask = sum(((way >> index) & 1) << bit for index, bit in enumerate(group))
            terms.append(permute(parts[way], mask))
    partial = functools.reduce(jnp.add, terms)
    user_grad = user_sums * grad_scale + decay_rate * user_factors.astype(jnp.float32)
    owned_rows = partial.shape[0]
    first_row = late * owned_rows
    chosen = lax.div(first_row, panel_rows) ^ lax.rem(late, panel_total)
    pieces = [lax.dynamic_slice_in_dim(panel, lax.rem(first_row, panel_rows), owned_rows, 0) for panel in panels]
    own_factors = pieces[0]
    for index in range(1, panel_total):
        own_factors = jnp.where(chosen == index, pieces[index], own_factors)
    item_grad = partial * grad_scale + decay_rate * own_factors.astype(jnp.float32)
    return (user_grad, item_grad)


def solution(mesh):
    in_specs = (
        P(AXES, None),
        P("items", None),
        P(AXES, None),
        P(AXES, None),
        P(AXES),
        P(AXES, None, None, None),
        P(AXES, None, None, None),
    )
    out_specs = (P(AXES, None), P(AXES, None))
    return jax.shard_map(body, mesh=mesh, in_specs=in_specs, out_specs=out_specs, check_vma=False)
```
